512 devices in a mesh: section: 16 (over y, core), tm: 32 (over x, z).
Axes of the slice: x: 4, y: 8, z: 8, core: 2. Of those that a mesh axis runs over, the one named last changes fastest.
Arguments:
- clips: bfloat16 [2, 32, 16, 8, 128], P(None, 'tm'), may hold values from -6 to 6
- kernels: bfloat16 [16, 3, 3, 3, 128, 128], P('section'), may hold values from -0.078125 to 0.078125
- cotangent: bfloat16 [2, 32, 16, 8, 128], P(None, 'tm'), may hold values from -6 to 6
Outputs:
- activations: bfloat16 [16, 2, 32, 16, 8, 128], P('section', None, 'tm')
- input_grads: bfloat16 [16, 2, 32, 16, 8, 128], P('section', None, 'tm')
- kernel_grads: float32 [16, 3, 3, 3, 128, 128], P('section')
The draws below stay inside these ranges and needn't reach their ends.
All inputs are finite; a program needn't handle non-finite values.
Results may differ from the reference program's by a relative error of at most 0.035.
Values may be sent and summed in bfloat16 or wider, within the bound.
A program may use at most 64 MiB of HBM per device.

```python
import jax
import jax.numpy as jnp
from jax import lax

C = 128
MICRO = 2
HEIGHT = 16
WIDTH = 8
SECTIONS = 16
FRAMES = 32


def block_levels(key, dims, shards, least, top_value):
    def one(axis_at, parts):
        heights = jax.random.uniform(jax.random.fold_in(jax.random.fold_in(key, 6), axis_at), (parts,), jnp.float32, least / len(shards), top_value / len(shards))
        return jnp.repeat(jnp.exp(heights), dims[axis_at] // parts).reshape((-1,) + (1,) * (len(dims) - axis_at - 1))

    loudness = one(*shards[0])
    for cut in shards[1:]:
        loudness = loudness * one(*cut)
    return loudness


def bell_draw(stream_key, extent, deviation, limit, pieces=(), held_as=jnp.bfloat16):
    level = block_levels(stream_key, extent, pieces, -0.22, 0.18) if pieces else 1.0
    values = jax.random.normal(stream_key, extent, jnp.float32) * deviation * level
    return jnp.minimum(jnp.maximum(values, -limit), limit).astype(held_as)


def setup_inputs(seed: int = 0) -> dict:
    splits = jax.random.split(jax.random.key(seed), 4)
    clips = bell_draw(splits[0], (MICRO, FRAMES, HEIGHT, WIDTH, C), 1.0, 6.0, ((1, 32),))
    kernels = bell_draw(splits[1], (SECTIONS, 3, 3, 3, C, C), (27 * C * 2) ** -0.5, 0.078125, ((0, 16),))
    cotangent = bell_draw(splits[2], (MICRO, FRAMES, HEIGHT, WIDTH, C), 1.0, 6.0, ((1, 32),))
    return {"clips": clips, "kernels": kernels, "cotangent": cotangent}


def conv_time(values, kernel, front, back):
    return lax.conv_general_dilated(values, kernel, (1, 1, 1), [(front, back), (1, 1), (1, 1)], dimension_numbers=('NDHWC', 'DHWIO', 'NDHWC'), preferred_element_type=jnp.float32)

def kernel_terms(silu_vals, grad_out):
    chan = silu_vals.shape[-1]
    frames = silu_vals.shape[1]
    height = silu_vals.shape[2]
    width = silu_vals.shape[3]
    padded = jnp.pad(silu_vals, ((0, 0), (2, 0), (1, 1), (1, 1), (0, 0)))
    flat_grad = grad_out.reshape(-1, chan)
    result = []
    for step_t in range(3):
        for step_h in range(3):
            for step_w in range(3):
                piece = padded[:, step_t:step_t + frames, step_h:step_h + height, step_w:step_w + width, :].reshape(-1, chan)
                result.append(lax.dot_general(piece, flat_grad, (((0,), (0,)), ((), ())), preferred_element_type=jnp.float32))
    return jnp.stack(result).reshape(3, 3, 3, chan, chan)

def reference(clips, kernels, cotangent):
    inputs = []
    outputs = []
    state = clips
    for layer in range(SECTIONS):
        inputs.append(state)
        silu_vals = jax.nn.silu(state.astype(jnp.float32)).astype(jnp.bfloat16)
        state = (state.astype(jnp.float32) + conv_time(silu_vals, kernels[layer], 2, 0)).astype(jnp.bfloat16)
        outputs.append(state)
    norm = 1.0 / jnp.sqrt(jnp.float32(MICRO * FRAMES * HEIGHT * WIDTH))
    grad_out = cotangent
    grads = [None] * SECTIONS
    kgrads = [None] * SECTIONS
    for layer in reversed(range(SECTIONS)):
        values = inputs[layer].astype(jnp.float32)
        silu_vals = jax.nn.silu(values).astype(jnp.bfloat16)
        flipped = jnp.swapaxes(kernels[layer][::-1, ::-1, ::-1], 3, 4)
        back_vals = conv_time(grad_out, flipped, 0, 2)
        logistic = jax.nn.sigmoid(values)
        deriv = logistic * (1.0 + values * (1.0 - logistic))
        kgrads[layer] = kernel_terms(silu_vals, grad_out) * norm
        grad_out = (grad_out.astype(jnp.float32) + back_vals * deriv).astype(jnp.bfloat16)
        grads[layer] = grad_out
    return (jnp.stack(outputs), jnp.stack(grads), jnp.stack(kgrads))
```

```python
import functools

import jax
import jax.numpy as jnp
from jax import lax
from jax.experimental import pallas as pl
from jax.experimental.pallas import tpu as pltpu
from jax.sharding import PartitionSpec as P

MESH = pl.DeviceIdType.MESH
PLANES = 8
ROWS = 112
BF16 = jnp.bfloat16
F32 = jnp.float32


def silu(v):
    return v / (1.0 + jnp.exp(-v))


def silu_slope(v):
    sig = 1.0 / (1.0 + jnp.exp(-v))
    return sig * (1.0 + v * (1.0 - sig))


def shift_w(a, d):
    r = pltpu.roll(a, (-d) % 8, 1)
    w = lax.broadcasted_iota(jnp.int32, a.shape, 1)
    return jnp.where(w < 7, r, 0.0) if d == 1 else jnp.where(w > 0, r, 0.0)


def shift_h(a, d):
    z = jnp.zeros((1,) + a.shape[1:], a.dtype)
    return jnp.concatenate([a[1:], z], axis=0) if d == 1 else jnp.concatenate([z, a[:-1]], axis=0)


def conv(frames, weight):
    count = len(frames) - 2
    rows = [jnp.concatenate(frames[f : f + 3], axis=1) for f in range(count)]
    left = jnp.concatenate(rows, axis=0) if count > 1 else rows[0]
    full = jnp.dot(left, weight[...], preferred_element_type=F32)
    outs = []
    for f in range(count):
        part = full[f * 128 : (f + 1) * 128]
        cols = []
        for dw in range(3):
            g = [part[:, (dh * 3 + dw) * 128 : (dh * 3 + dw + 1) * 128].reshape(16, 8, 128) for dh in range(3)]
            cols.append(g[1] + shift_h(g[0], -1) + shift_h(g[2], 1))
        acc = cols[1] + shift_w(cols[0], -1) + shift_w(cols[2], 1)
        outs.append(acc.reshape(128, 128))
    return outs


def tm_of(m, j):
    x = j // 4
    a = j % 4
    return x * 8 + 4 * m + a + (x % 2) * (3 - 2 * a)


def kernel(
    clips, k_ref, cot, act, grad, kg,
    X0, X1, X2, G2, G1, G0, BK, Kraw, WfA, WfB, WbA, WbB, TT, PX, KX, GL, RS, RL,
    SS, x0r, g2r, kr, kxr, acr, grr, pxr, glr, rsr, azr, axr,
):
    s = lax.axis_index("section")
    t = lax.axis_index("tm")
    y = s // 2
    c = s % 2
    x = t // 8
    z = t % 8
    m = z // 4
    a = z % 4
    j = 4 * x + a + (x % 2) * (3 - 2 * a)
    q = t // 2
    e = t % 2
    first = c == 0
    second = c == 1
    drains = []

    def remote(src, dst, recv, dev, idx):
        return pltpu.make_async_remote_copy(
            src_ref=src, dst_ref=dst, send_sem=SS.at[idx], recv_sem=recv, device_id=dev, device_id_type=MESH
        )

    def send(src, dst, recv, dev, cond=None):
        idx = len(drains)
        make = lambda: remote(src, dst, recv, dev, idx)
        if cond is None:
            make().start()
        else:
            pl.when(cond)(lambda: make().start())
        drains.append((cond, make))

    def send_or_copy(src, dst, recv, dev, cond, own):
        send(src, dst, recv, dev, jnp.logical_and(cond, jnp.logical_not(own)))

        @pl.when(jnp.logical_and(cond, own))
        def _():
            pltpu.make_async_copy(src, dst, recv).start()

    def arrive(dst, recv):
        pltpu.make_async_remote_copy(
            src_ref=dst, dst_ref=dst, send_sem=SS.at[0], recv_sem=recv,
            device_id=(s - c + (1 - c), t), device_id_type=MESH,
        ).wait_recv()

    def arrive_if(cond, dst, recv):
        pl.when(cond)(lambda: arrive(dst, recv))

    both = jnp.logical_and

    for dj in (2, 1, 0, -1):
        for mm in range(2):
            there = q + dj
            ok = both(both(second, y == 0), both(there >= 0, there <= 15))
            to = tm_of(mm, there)
            send_or_copy(
                clips.at[mm], X0.at[(2 - dj) * 2 + e], x0r.at[2 - dj], (1, to), ok, to == t
            )
    send(k_ref, Kraw, kr, (s + 1, t), first)
    for dj in (0, -1, -2):
        for mm in range(2):
            there = q + dj
            ok = both(both(first, y == PLANES - 1), both(there >= 0, there <= 15))
            send(cot.at[mm], G2.at[-2 * dj + e], g2r.at[-dj], (2 * PLANES - 1, tm_of(mm, there)), ok)

    def fwd_weight(dst, src):
        for tap in range(27):
            dt, n = tap // 9, tap % 9
            dst[dt * 128 : (dt + 1) * 128, n * 128 : (n + 1) * 128] = src[tap]

    def bwd_weight(dst, src):
        for tap in range(27):
            dt, n = tap // 9, tap % 9
            dst[dt * 128 : (dt + 1) * 128, n * 128 : (n + 1) * 128] = src[26 - tap].astype(F32).T.astype(BF16)

    def frame_silu(ref, k):
        return silu(ref[k].astype(F32)).astype(BF16)

    def build_patches(ref, base):
        def one(k, carry):
            v = frame_silu(ref, base + k).astype(F32).reshape(16, 8, 128)
            for dw in range(3):
                vw = v if dw == 1 else shift_w(v, dw - 1)
                for dh in range(3):
                    vh = vw if dh == 1 else shift_h(vw, dh - 1)
                    TT[k, dh * 3 + dw] = vh.reshape(128, 128).T.astype(BF16)
            return carry

        lax.fori_loop(0, 4, one, 0)

    def block_a(lo, hi):
        out = conv([frame_silu(X0, k) for k in range(lo, hi + 2)], WfA)
        for k in range(lo, hi):
            X1[k] = (X0[k + 2].astype(F32) + out[k - lo]).astype(BF16)

    def block_b():
        out = conv([frame_silu(X1, k) for k in range(4)], WfB)
        for k in range(2):
            X2[k] = (X1[k + 2].astype(F32) + out[k]).astype(BF16)

    def back_a():
        out = conv([G2[k] for k in range(6)], WbB)
        for k in range(4):
            BK[k] = out[k]

    def out_home(src, dst, recv, core):
        for k in range(2):
            dev = (2 * y + core, 2 * j + k)
            if core == 0:
                send(src.at[k], dst.at[m], recv.at[m], dev, second)
            else:
                send_or_copy(src.at[k], dst.at[m], recv.at[m], dev, second, 2 * j + k == t)

    @pl.when(second)
    def _():
        zero2 = jnp.zeros((2, 128, 128), BF16)

        @pl.when(j < 2)
        def _():
            X0[0:2] = zero2

        @pl.when(j < 1)
        def _():
            X0[2:4] = zero2

        @pl.when(j > 14)
        def _():
            X0[6:8] = zero2
            G2[2:4] = zero2

        @pl.when(j > 13)
        def _():
            G2[4:6] = zero2

        fwd_weight(WfB, k_ref)
        arrive(Kraw, kr)
        fwd_weight(WfA, Kraw)

        @pl.when(y > 0)
        def _():
            bwd_weight(WbB, k_ref)
            bwd_weight(WbA, Kraw)

        @pl.when(y == PLANES - 1)
        def _():
            arrive(G2.at[0:2], g2r.at[0])
            arrive_if(j <= 14, G2.at[2:4], g2r.at[1])
            arrive_if(j <= 13, G2.at[4:6], g2r.at[2])
            back_a()

        arrive(X0.at[4:6], x0r.at[2])
        arrive_if(j >= 1, X0.at[2:4], x0r.at[1])

        @pl.when(y < PLANES - 1)
        def _():
            arrive_if(j >= 2, X0.at[0:2], x0r.at[0])
            block_a(0, 4)
            block_b()

        @pl.when(y == PLANES - 1)
        def _():
            arrive_if(j <= 14, X0.at[6:8], x0r.at[3])
            block_a(2, 6)

    for dj in (2, 1, 0, -1):
        there = j + dj
        ok = both(both(second, y < PLANES - 1), both(there >= 0, there <= 15))
        send(X2, X0.at[(2 - dj) * 2 : (2 - dj) * 2 + 2], x0r.at[2 - dj], (s + 2, tm_of(m, there)), ok)

    early = both(second, y < PLANES - 2)
    late = both(second, y >= PLANES - 2)

    @pl.when(both(second, y == 0))
    def _():
        bwd_weight(WbB, k_ref)
        bwd_weight(WbA, Kraw)

    @pl.when(both(second, y < PLANES - 1))
    def _():
        arrive_if(j <= 14, X0.at[6:8], x0r.at[3])
        block_a(4, 6)

    def swap_patches(cond):
        for d in range(4):
            other = (x + d) % 4
            src = TT.at[:, :, pl.ds(pl.multiple_of(32 * other, 32), 32), :]
            if d == 0:
                pl.when(cond)(lambda: pltpu.make_async_copy(src, PX.at[x], pxr.at[0]).start())
            else:
                send(src, PX.at[x], pxr.at[d], (s, other * 8 + z), cond)

    @pl.when(early)
    def _():
        build_patches(X1, 0)

    swap_patches(early)

    @pl.when(second)
    def _():
        @pl.when(y < PLANES - 1)
        def _():
            arrive(G2.at[0:2], g2r.at[0])
            arrive_if(j <= 14, G2.at[2:4], g2r.at[1])
            arrive_if(j <= 13, G2.at[4:6], g2r.at[2])
            back_a()

        for k in range(4):
            G1[k] = (G2[k].astype(F32) + BK[k] * silu_slope(X1[k + 2].astype(F32))).astype(BF16)
        out = conv([G1[k] for k in range(4)], WbA)
        for k in range(2):
            G0[k] = (G1[k].astype(F32) + out[k] * silu_slope(X0[k + 4].astype(F32))).astype(BF16)

    for dj in (-2, -1, 0):
        there = j + dj
        ok = both(both(second, y > 0), there >= 0)
        send(G0, G2.at[-2 * dj : -2 * dj + 2], g2r.at[-dj], (s - 2, tm_of(m, there)), ok)
    for d in range(4):
        other = (x + d) % 4
        send(G1.at[0:2], GL.at[x], glr.at[d], (s - 1, other * 8 + z), second)
    for d in range(1, 4):
        other = (x + d) % 4
        send(G2.at[0:2], GL.at[x], glr.at[d], (s, other * 8 + z), second)
    pl.when(second)(lambda: pltpu.make_async_copy(G2.at[0:2], GL.at[x], glr.at[0]).start())
    send(X0.at[2:6], KX, kxr, (s - 1, t), second)
    out_home(G0, grad, grr, 0)
    out_home(G1, grad, grr, 1)

    @pl.when(both(second, y == PLANES - 1))
    def _():
        arrive_if(j >= 2, X0.at[0:2], x0r.at[0])
        block_a(0, 2)
        block_b()

    out_home(X1.at[2:4], act, acr, 0)
    out_home(X2, act, acr, 1)

    @pl.when(first)
    def _():
        arrive(KX, kxr)
        build_patches(KX, 0)

    @pl.when(late)
    def _():
        build_patches(X1, 0)

    swap_patches(jnp.logical_or(first, late))

    for d in range(4):
        source = (x + 4 - d) % 4
        arrive(PX.at[source], pxr.at[d])
        arrive(GL.at[source], glr.at[d])
    for dt in range(3):
        total = None
        for p in range(4):
            left = jnp.concatenate(
                [PX[p, dt].reshape(288, 128), PX[p, dt + 1].reshape(288, 128)], axis=1
            )
            term = jnp.dot(left, GL[p].reshape(256, 128), preferred_element_type=F32)
            total = term if total is None else total + term
        RS[dt * 288 : (dt + 1) * 288, :] = total.astype(BF16)
    RS[864:896, :] = jnp.zeros((32, 128), BF16)

    def chunk(k):
        return pl.ds(pl.multiple_of(k * ROWS, 16), ROWS)

    for d in range(1, 8):
        other = (z + d) % 8
        send(RS.at[chunk(other)], RL.at[z], rsr.at[d], (s, x * 8 + other))
    total = RS[chunk(z), :].astype(F32)
    for d in range(1, 8):
        source = (z + 8 - d) % 8
        arrive(RL.at[source], rsr.at[d])
        total = total + RL[source].astype(F32)
    mine = kg.at[x, chunk(z)]
    mine[...] = total.astype(BF16)
    for d in range(1, 8):
        other = (z + d) % 8
        send(mine, mine, azr.at[d], (s, x * 8 + other))
    for d in range(1, 8):
        source = (z + 8 - d) % 8
        arrive(kg.at[x, chunk(source)], azr.at[d])
    for d in range(1, 4):
        other = (x + d) % 4
        send(kg.at[x], kg.at[x], axr.at[d], (s, other * 8 + z))
    for d in range(1, 4):
        source = (x + 4 - d) % 4
        arrive(kg.at[source], axr.at[d])
    for mm in range(2):
        arrive(act.at[mm], acr.at[mm])
        arrive(grad.at[mm], grr.at[mm])
    for cond, make in drains:
        if cond is None:
            make().wait_send()
        else:
            pl.when(cond)(lambda make=make: make().wait_send())


def body(clips, kernels, cotangent):
    micro, frames, height, width, chan = clips.shape
    vmem = pl.BlockSpec(memory_space=pltpu.VMEM)
    frame = lambda n: pltpu.VMEM((n, 128, 128), BF16)
    weight = pltpu.VMEM((384, 1152), BF16)
    dma = pltpu.SemaphoreType.DMA
    act, grad, kg = pl.pallas_call(
        kernel,
        out_shape=(
            jax.ShapeDtypeStruct((2, 128, 128), BF16),
            jax.ShapeDtypeStruct((2, 128, 128), BF16),
            jax.ShapeDtypeStruct((4, 8 * ROWS, 128), BF16),
        ),
        in_specs=[vmem] * 3,
        out_specs=(vmem,) * 3,
        scratch_shapes=[
            frame(8), frame(6), frame(2), frame(6), frame(4), frame(2),
            pltpu.VMEM((4, 128, 128), F32),
            frame(27), weight, weight, weight, weight,
            pltpu.VMEM((4, 9, 128, 128), BF16),
            pltpu.VMEM((4, 4, 9, 32, 128), BF16),
            frame(4),
            pltpu.VMEM((4, 2, 128, 128), BF16),
            pltpu.VMEM((8 * ROWS, 128), BF16),
            pltpu.VMEM((8, ROWS, 128), BF16),
            dma((80,)), dma((4,)), dma((3,)), dma, dma, dma((2,)), dma((2,)),
            dma((4,)), dma((4,)), dma((8,)), dma((8,)), dma((4,)),
        ],
        compiler_params=pltpu.CompilerParams(has_side_effects=True, vmem_limit_bytes=48 << 20),
        name="blocks",
    )(
        clips.reshape(2, 128, 128),
        kernels.reshape(27, 128, 128),
        cotangent.reshape(2, 128, 128),
    )
    total = micro * frames * lax.axis_size("tm") * height * width
    norm = 1.0 / jnp.sqrt(jnp.float32(total))
    parts = kg[:, :864].reshape(4, 27, 32, 128).transpose(1, 0, 2, 3).astype(F32) * norm
    return (
        act.reshape(1, micro, 1, height, width, chan),
        grad.reshape(1, micro, 1, height, width, chan),
        parts.reshape(1, 3, 3, 3, chan, chan),
    )


def solution(mesh):
    placed = (
        P(None, "tm", None, None, None),
        P("section", None, None, None, None, None),
        P(None, "tm", None, None, None),
    )
    return jax.shard_map(
        body,
        mesh=mesh,
        in_specs=placed,
        out_specs=(
            P("section", None, "tm", None, None, None),
            P("section", None, "tm", None, None, None),
            P("section", None, None, None, None, None),
        ),
        check_vma=False,
    )
```

```python
import functools

import jax
import jax.numpy as jnp
from jax import lax
from jax.experimental import pallas as pl
from jax.experimental.pallas import tpu as pltpu
from jax.sharding import PartitionSpec as P

MESH = pl.DeviceIdType.MESH
PLANES = 8
ROWS = 112
BF16 = jnp.bfloat16
F32 = jnp.float32


def logistic(v):
    return 0.5 + 0.5 * jnp.tanh(0.5 * v)


def silu(v):
    return v * logistic(v)


def silu_slope(v):
    sig = logistic(v)
    return sig * (1.0 + v * (1.0 - sig))


def shift_w(a, d):
    r = pltpu.roll(a, (-d) % 8, 1)
    w = lax.broadcasted_iota(jnp.int32, a.shape, 1)
    return jnp.where(w < 7, r, 0.0) if d == 1 else jnp.where(w > 0, r, 0.0)


def shift_h(a, d):
    z = jnp.zeros((1,) + a.shape[1:], a.dtype)
    return jnp.concatenate([a[1:], z], axis=0) if d == 1 else jnp.concatenate([z, a[:-1]], axis=0)


def conv(frames, weight):
    count = len(frames) - 2
    rows = [jnp.concatenate(frames[f : f + 3], axis=1) for f in range(count)]
    left = jnp.concatenate(rows, axis=0) if count > 1 else rows[0]
    full = jnp.dot(left, weight[...], preferred_element_type=F32)
    outs = []
    for f in range(count):
        part = full[f * 128 : (f + 1) * 128]
        cols = []
        for dw in range(3):
            g = [part[:, (dh * 3 + dw) * 128 : (dh * 3 + dw + 1) * 128].reshape(16, 8, 128) for dh in range(3)]
            cols.append(g[1] + shift_h(g[0], -1) + shift_h(g[2], 1))
        acc = cols[1] + shift_w(cols[0], -1) + shift_w(cols[2], 1)
        outs.append(acc.reshape(128, 128))
    return outs


def tm_of(m, j):
    b, xx = j // 8, j % 8 // 2
    return (xx + b * (3 - 2 * xx)) * 8 + 4 * m + 2 * b + j % 2


def kernel(
    clips, k_hbm, cot, act, grad, kg,
    X0, X1, X2, G2, G1, G0, BK, S1, S0, WfA, WfB, WbA, WbB, KX, AG,
    TT, PX, GL, RS, RL, TT2, PX2, GL2, RS2, RL2,
    SS, ownr, x0r, g2r, kr, kxr, acr, grr, pxr, glr, rsr, px2r, gl2r, rs2r, kgr, azr, axr, az2r, ax2r,
):
    s = lax.axis_index("section")
    t = lax.axis_index("tm")
    y = s // 2
    c = s % 2
    x = t // 8
    z = t % 8
    m = z // 4
    b = z % 4 // 2
    j = 8 * b + 2 * (x + b * (3 - 2 * x)) + z % 2
    q = t // 2
    e = t % 2
    first = c == 0
    second = c == 1
    drains = []
    both = jnp.logical_and

    def remote(src, dst, recv, dev, idx):
        return pltpu.make_async_remote_copy(
            src_ref=src, dst_ref=dst, send_sem=SS.at[idx], recv_sem=recv, device_id=dev, device_id_type=MESH
        )

    def send(src, dst, recv, dev, cond=None):
        idx = len(drains)
        make = lambda: remote(src, dst, recv, dev, idx)
        if cond is None:
            make().start()
        else:
            pl.when(cond)(lambda: make().start())
        drains.append((cond, make))

    def send_or_copy(src, dst, recv, dev, cond, own):
        send(src, dst, recv, dev, jnp.logical_and(cond, jnp.logical_not(own)))

        @pl.when(jnp.logical_and(cond, own))
        def _():
            pltpu.make_async_copy(src, dst, recv).start()

    def arrive(dst, recv):
        pltpu.make_async_remote_copy(
            src_ref=dst, dst_ref=dst, send_sem=SS.at[0], recv_sem=recv,
            device_id=(s - c + (1 - c), t), device_id_type=MESH,
        ).wait_recv()

    def arrive_if(cond, dst, recv):
        pl.when(cond)(lambda: arrive(dst, recv))

    def tap_block(ref, tap):
        dt, n = tap // 9, tap % 9
        return ref.at[dt * 128 : (dt + 1) * 128, n * 128 : (n + 1) * 128]

    @pl.when(second)
    def _():
        for tap in range(27):
            pltpu.make_async_copy(k_hbm.at[tap], tap_block(WfB, tap), ownr).start()

    entry = pltpu.get_barrier_semaphore()
    expected = []

    def greet(cond, dev):
        pl.when(cond)(lambda: pl.semaphore_signal(entry, inc=1, device_id=dev, device_id_type=MESH))

    def expect(cond):
        expected.append(cond.astype(jnp.int32))

    inside = lambda v, top: both(v >= 0, v <= top)
    for k in range(-4, 4):
        at = 2 * j + k
        greet(both(both(second, y == 0), both(inside(at, 31), at != t)), (1, at))
    for dj in (2, 1, 0, -1):
        for mm in range(2):
            ok = both(both(second, y == 0), inside(q + dj, 15))
            expect(both(ok, tm_of(mm, q + dj) != t))
    for dj in (2, 1, 0, -1):
        greet(both(both(second, y > 0), inside(j - dj, 15)), (s - 2, tm_of(m, j - dj)))
        expect(both(both(second, y < PLANES - 1), inside(j + dj, 15)))
    for dj in (-2, -1, 0):
        greet(both(both(second, y < PLANES - 1), inside(j - dj, 15)), (s + 2, tm_of(m, j - dj)))
        expect(both(both(second, y > 0), inside(j + dj, 15)))
    for k in range(6):
        at = 2 * j + k
        greet(both(both(second, y == PLANES - 1), at <= 31), (2 * PLANES - 2, at))
    for dj in (0, -1, -2):
        for mm in range(2):
            expect(both(both(first, y == PLANES - 1), inside(q + dj, 15)))
    always = s >= 0
    for d in range(4):
        greet(first, (s + 1, (x + d) % 4 * 8 + z))
        expect(second)
    greet(second, (s - 1, t))
    expect(first)
    greet(both(first, y > 0), (s - 1, t))
    expect(both(second, y < PLANES - 1))
    greet(both(second, y < PLANES - 1), (s + 1, t))
    expect(both(first, y > 0))
    for d in range(1, 4):
        greet(always, (s, (x + d) % 4 * 8 + z))
        expect(always)
    for d in range(1, 8):
        greet(always, (s, x * 8 + (z + d) % 8))
        expect(always)
    for mm in range(2):
        at = tm_of(mm, q)
        greet(jnp.logical_or(first, at != t), (2 * y + 1, at))
    for k in range(2):
        expect(second)
        expect(both(second, 2 * j + k != t))
    pl.semaphore_wait(entry, sum(expected))

    for dj in (2, 1, 0, -1):
        for mm in range(2):
            there = q + dj
            ok = both(both(second, y == 0), both(there >= 0, there <= 15))
            to = tm_of(mm, there)
            send_or_copy(
                clips.at[mm], X0.at[(2 - dj) * 2 + e], x0r.at[2 - dj], (1, to), ok, to == t
            )
    idx = len(drains)
    all_taps = lambda: remote(k_hbm, k_hbm, kr, (s + 1, t), idx)
    drains.append((first, all_taps))

    @pl.when(first)
    def _():
        for tap in range(27):
            remote(k_hbm.at[tap], tap_block(WfA, tap), kr, (s + 1, t), idx).start()

    for dj in (0, -1, -2):
        for mm in range(2):
            there = q + dj
            ok = both(both(first, y == PLANES - 1), both(there >= 0, there <= 15))
            send(cot.at[mm], G2.at[-2 * dj + e], g2r.at[-dj], (2 * PLANES - 1, tm_of(mm, there)), ok)

    def bwd_weight(dst, src):
        for tap in range(27):
            tap_block(dst, tap)[...] = tap_block(src, 26 - tap)[...].astype(F32).T.astype(BF16)

    def frame_silu(ref, k):
        return silu(ref[k].astype(F32)).astype(BF16)

    def build_patches(ref, TT):
        def one(k, carry):
            v = frame_silu(ref, k).astype(F32).reshape(16, 8, 128)
            for dw in range(3):
                vw = v if dw == 1 else shift_w(v, dw - 1)
                for dh in range(3):
                    vh = vw if dh == 1 else shift_h(vw, dh - 1)
                    TT[k, dh * 3 + dw] = vh.reshape(128, 128).T.astype(BF16)
            return carry

        lax.fori_loop(0, 4, one, 0)

    def block_a(lo, hi):
        out = conv([frame_silu(X0, k) for k in range(lo, hi + 2)], WfA)
        for k in range(lo, hi):
            X1[k] = (X0[k + 2].astype(F32) + out[k - lo]).astype(BF16)

    def block_b():
        out = conv([frame_silu(X1, k) for k in range(4)], WfB)
        for k in range(2):
            X2[k] = (X1[k + 2].astype(F32) + out[k]).astype(BF16)

    def back_a():
        out = conv([G2[k] for k in range(6)], WbB)
        for k in range(4):
            BK[k] = out[k]

    def out_home(src, dst, recv, core, cond):
        for k in range(2):
            dev = (2 * y + core, 2 * j + k)
            if core == 0:
                send(src.at[k], dst.at[m], recv.at[m], dev, cond)
            else:
                send_or_copy(src.at[k], dst.at[m], recv.at[m], dev, cond, 2 * j + k == t)

    @pl.when(second)
    def _():
        zero2 = jnp.zeros((2, 128, 128), BF16)

        @pl.when(j < 2)
        def _():
            X0[0:2] = zero2

        @pl.when(j < 1)
        def _():
            X0[2:4] = zero2

        @pl.when(j > 14)
        def _():
            X0[6:8] = zero2
            G2[2:4] = zero2

        @pl.when(j > 13)
        def _():
            G2[4:6] = zero2

        pltpu.make_async_copy(WfB, WfB, ownr).wait()
        arrive(WfA, kr)

        @pl.when(y > 0)
        def _():
            bwd_weight(WbB, WfB)
            bwd_weight(WbA, WfA)

        @pl.when(y == PLANES - 1)
        def _():
            arrive(G2.at[0:2], g2r.at[0])
            arrive_if(j <= 14, G2.at[2:4], g2r.at[1])
            arrive_if(j <= 13, G2.at[4:6], g2r.at[2])
            back_a()

        arrive(X0.at[4:6], x0r.at[2])
        arrive_if(j >= 1, X0.at[2:4], x0r.at[1])

        @pl.when(y < PLANES - 1)
        def _():
            arrive_if(j >= 2, X0.at[0:2], x0r.at[0])
            block_a(0, 4)
            block_b()

        @pl.when(y == PLANES - 1)
        def _():
            arrive_if(j <= 14, X0.at[6:8], x0r.at[3])
            block_a(2, 6)

    forward = both(second, y < PLANES - 1)
    fast = []

    def flush():
        while fast:
            cond, make = fast.pop()
            pl.when(cond)(lambda make=make: make().wait_send())

    def send_fast(src, dst, recv, dev, cond):
        send(src, dst, recv, dev, cond)
        fast.append(drains[-1])
        drains[-1] = None

    for dj in (2, 1, 0, -1):
        there = j + dj
        ok = both(forward, inside(there, 15))
        send_fast(X2, X0.at[(2 - dj) * 2 : (2 - dj) * 2 + 2], x0r.at[2 - dj], (s + 2, tm_of(m, there)), ok)

    top = both(second, y == PLANES - 1)

    @pl.when(both(second, y == 0))
    def _():
        bwd_weight(WbB, WfB)
        bwd_weight(WbA, WfA)

    @pl.when(both(second, y < PLANES - 1))
    def _():
        arrive_if(j <= 14, X0.at[6:8], x0r.at[3])
        block_a(4, 6)

    flush()
    send(X1.at[0:4], KX, kxr, (s + 1, t), forward)

    def swap_patches(cond, TT, PX, pxr):
        for d in range(4):
            other = (x + d) % 4
            src = TT.at[:, :, pl.ds(pl.multiple_of(32 * other, 32), 32), :]
            if d == 0:
                pl.when(cond)(lambda: pltpu.make_async_copy(src, PX.at[x], pxr.at[0]).start())
            else:
                send(src, PX.at[x], pxr.at[d], (s, other * 8 + z), cond)

    @pl.when(forward)
    def _():
        build_patches(X0.at[2:6], TT)

    swap_patches(forward, TT, PX, pxr)
    out_home(X1.at[2:4], act, acr, 0, forward)
    out_home(X2, act, acr, 1, forward)

    @pl.when(second)
    def _():
        for k in range(4):
            S1[k] = silu_slope(X1[k + 2].astype(F32))
        for k in range(2):
            S0[k] = silu_slope(X0[k + 4].astype(F32))

        @pl.when(y < PLANES - 1)
        def _():
            arrive(G2.at[0:2], g2r.at[0])
            arrive_if(j <= 14, G2.at[2:4], g2r.at[1])
            arrive_if(j <= 13, G2.at[4:6], g2r.at[2])
            back_a()

        for k in range(4):
            G1[k] = (G2[k].astype(F32) + BK[k] * S1[k]).astype(BF16)

    def gather(src, GL, glr, cond):
        for d in (2, 1, 3):
            other = (x + d) % 4
            send(src, GL.at[x], glr.at[d], (s, other * 8 + z), cond)
        pl.when(cond)(lambda: pltpu.make_async_copy(src, GL.at[x], glr.at[0]).start())

    gather(G1.at[0:2], GL, glr, both(second, y == 0))

    @pl.when(second)
    def _():
        out = conv([G1[k] for k in range(4)], WbA)
        for k in range(2):
            G0[k] = (G1[k].astype(F32) + out[k] * S0[k]).astype(BF16)

    for dj in (-2, -1, 0):
        there = j + dj
        ok = both(both(second, y > 0), there >= 0)
        send_fast(G0, G2.at[-2 * dj : -2 * dj + 2], g2r.at[-dj], (s - 2, tm_of(m, there)), ok)
    flush()
    behind = both(second, y > 0)
    for d in (2, 1, 3, 0):
        other = (x + d) % 4
        send(G0, GL.at[x], glr.at[d], (s - 1, other * 8 + z), behind)
    gather(G1.at[0:2], GL, glr, behind)
    gather(G2.at[0:2], GL2, gl2r, top)
    out_home(G0, grad, grr, 0, second)
    out_home(G1, grad, grr, 1, second)

    @pl.when(top)
    def _():
        arrive_if(j >= 2, X0.at[0:2], x0r.at[0])
        block_a(0, 2)
        block_b()
        build_patches(X0.at[2:6], TT)
        build_patches(X1, TT2)

    out_home(X1.at[2:4], act, acr, 0, top)
    out_home(X2, act, acr, 1, top)
    swap_patches(top, TT2, PX2, px2r)

    lower = both(first, y > 0)

    @pl.when(lower)
    def _():
        arrive(KX, kxr)
        build_patches(KX, TT)

    swap_patches(jnp.logical_or(lower, top), TT, PX, pxr)

    def chunk(k):
        return pl.ds(pl.multiple_of(k * ROWS, 16), ROWS)

    def reduce_terms(cond, PX, GL, RS, RL, pxr, glr, rsr, out):
        @pl.when(cond)
        def _():
            for d in range(4):
                source = (x + 4 - d) % 4
                arrive(PX.at[source], pxr.at[d])
                arrive(GL.at[source], glr.at[d])
            for dt in range(3):
                total = None
                for p in range(4):
                    left = jnp.concatenate(
                        [PX[p, dt].reshape(288, 128), PX[p, dt + 1].reshape(288, 128)], axis=1
                    )
                    term = jnp.dot(left, GL[p].reshape(256, 128), preferred_element_type=F32)
                    total = term if total is None else total + term
                RS[dt * 288 : (dt + 1) * 288, :] = total.astype(BF16)
            RS[864:896, :] = jnp.zeros((32, 128), BF16)

        for d in (4, 3, 5, 2, 6, 1, 7):
            other = (z + d) % 8
            send(RS.at[chunk(other)], RL.at[z], rsr.at[d], (s, x * 8 + other), cond)

        @pl.when(cond)
        def _():
            total = RS[chunk(z), :].astype(F32)
            for d in range(1, 8):
                source = (z + 8 - d) % 8
                arrive(RL.at[source], rsr.at[d])
                total = total + RL[source].astype(F32)
            out[...] = total.astype(BF16)

    right, left, far = (x + 1) % 4, (x + 3) % 4, (x + 2) % 4
    order = (0, 1, 7, 2, 6, 3, 5, 4)

    def gather_sum(cond, buf, azr, axr, deliver):
        piece = lambda ref, row, d: ref.at[row, chunk((z + 8 - d) % 8)]

        def pass_on(row, d, recv, dev):
            send(piece(buf, row, d), piece(buf, row, d), recv, dev, cond)

        def hand_over(row, d):
            if deliver:
                send(piece(buf, row, d), piece(kg, row, d), kgr, (s - 1, t), cond)

        for d in (4, 3, 5, 2, 6, 1, 7):
            pass_on(x, 0, azr.at[d], (s, x * 8 + (z + d) % 8))
        for d in order:
            if d:
                arrive_if(cond, piece(buf, x, d), azr.at[d])
            pass_on(x, d, axr.at[0, d], (s, right * 8 + z))
            pass_on(x, d, axr.at[1, d], (s, left * 8 + z))
        for at, d in enumerate(order):
            arrive_if(cond, piece(buf, left, d), axr.at[0, d])
            arrive_if(cond, piece(buf, right, d), axr.at[1, d])
            if at % 2:
                pass_on(left, d, axr.at[2, d], (s, right * 8 + z))
            else:
                pass_on(right, d, axr.at[2, d], (s, left * 8 + z))
            hand_over(x, d)
        for d in order:
            hand_over(left, d)
            hand_over(right, d)
        for d in order:
            arrive_if(cond, piece(buf, far, d), axr.at[2, d])
            hand_over(far, d)

    working = s > 0
    reduce_terms(working, PX, GL, RS, RL, pxr, glr, rsr, AG.at[x, chunk(z)])
    gather_sum(working, AG, azr, axr, True)
    reduce_terms(top, PX2, GL2, RS2, RL2, px2r, gl2r, rs2r, kg.at[x, chunk(z)])
    gather_sum(top, kg, az2r, ax2r, False)
    arrive_if(s < 2 * PLANES - 1, kg, kgr)
    for mm in range(2):
        arrive(act.at[mm], acr.at[mm])
        arrive(grad.at[mm], grr.at[mm])
    for cond, make in filter(None, drains):
        if cond is None:
            make().wait_send()
        else:
            pl.when(cond)(lambda make=make: make().wait_send())


def body(clips, kernels, cotangent):
    micro, frames, height, width, chan = clips.shape
    vmem = pl.BlockSpec(memory_space=pltpu.VMEM)
    frame = lambda n: pltpu.VMEM((n, 128, 128), BF16)
    weight = pltpu.VMEM((384, 1152), BF16)
    dma = pltpu.SemaphoreType.DMA
    terms = (
        pltpu.VMEM((4, 9, 128, 128), BF16),
        pltpu.VMEM((4, 4, 9, 32, 128), BF16),
        pltpu.VMEM((4, 2, 128, 128), BF16),
        pltpu.VMEM((8 * ROWS, 128), BF16),
        pltpu.VMEM((8, ROWS, 128), BF16),
    )
    act, grad, kg = pl.pallas_call(
        kernel,
        out_shape=(
            jax.ShapeDtypeStruct((2, 128, 128), BF16),
            jax.ShapeDtypeStruct((2, 128, 128), BF16),
            jax.ShapeDtypeStruct((4, 8 * ROWS, 128), BF16),
        ),
        in_specs=[pl.BlockSpec(memory_space=pl.ANY)] * 3,
        out_specs=(vmem,) * 3,
        scratch_shapes=[
            frame(8), frame(6), frame(2), frame(6), frame(4), frame(2),
            pltpu.VMEM((4, 128, 128), F32),
            pltpu.VMEM((4, 128, 128), F32),
            pltpu.VMEM((2, 128, 128), F32),
            weight, weight, weight, weight, frame(4), pltpu.VMEM((4, 8 * ROWS, 128), BF16),
            *terms, *terms,
            dma((210,)), dma, dma((4,)), dma((3,)), dma, dma, dma((2,)), dma((2,)),
            dma((4,)), dma((4,)), dma((8,)), dma((4,)), dma((4,)), dma((8,)),
            dma, dma((8,)), dma((3, 8)), dma((8,)), dma((3, 8)),
        ],
        compiler_params=pltpu.CompilerParams(
            collective_id=0, has_side_effects=True, vmem_limit_bytes=48 << 20,
        ),
        name="blocks",
    )(
        clips.reshape(2, 128, 128),
        kernels.reshape(27, 128, 128),
        cotangent.reshape(2, 128, 128),
    )
    total = micro * frames * lax.axis_size("tm") * height * width
    norm = 1.0 / jnp.sqrt(jnp.float32(total))
    parts = kg[:, :864].reshape(4, 27, 32, 128).transpose(1, 0, 2, 3).astype(F32) * norm
    return (
        act.reshape(1, micro, 1, height, width, chan),
        grad.reshape(1, micro, 1, height, width, chan),
        parts.reshape(1, 3, 3, 3, chan, chan),
    )


def solution(mesh):
    placed = (
        P(None, "tm", None, None, None),
        P("section", None, None, None, None, None),
        P(None, "tm", None, None, None),
    )
    return jax.shard_map(
        body,
        mesh=mesh,
        in_specs=placed,
        out_specs=(
            P("section", None, "tm", None, None, None),
            P("section", None, "tm", None, None, None),
            P("section", None, None, None, None, None),
        ),
        check_vma=False,
    )
```

```python
import functools

import jax
import jax.numpy as jnp
from jax import lax
from jax.experimental import pallas as pl
from jax.experimental.pallas import tpu as pltpu
from jax.sharding import PartitionSpec as P

MESH = pl.DeviceIdType.MESH
PLANES = 8
ROWS = 112
BF16 = jnp.bfloat16
F32 = jnp.float32


def logistic(v):
    return 0.5 + 0.5 * jnp.tanh(0.5 * v)


def silu(v):
    return v * logistic(v)


def silu_slope(v):
    sig = logistic(v)
    return sig * (1.0 + v * (1.0 - sig))


def shift_w(a, d):
    r = pltpu.roll(a, (-d) % 8, 1)
    w = lax.broadcasted_iota(jnp.int32, a.shape, 1)
    return jnp.where(w < 7, r, 0.0) if d == 1 else jnp.where(w > 0, r, 0.0)


def shift_h(a, d):
    z = jnp.zeros((1,) + a.shape[1:], a.dtype)
    return jnp.concatenate([a[1:], z], axis=0) if d == 1 else jnp.concatenate([z, a[:-1]], axis=0)


def conv(frames, weight):
    count = len(frames) - 2
    rows = [jnp.concatenate(frames[f : f + 3], axis=1) for f in range(count)]
    left = jnp.concatenate(rows, axis=0) if count > 1 else rows[0]
    full = jnp.dot(left, weight[...], preferred_element_type=F32)
    outs = []
    for f in range(count):
        part = full[f * 128 : (f + 1) * 128]
        cols = []
        for dw in range(3):
            g = [part[:, (dh * 3 + dw) * 128 : (dh * 3 + dw + 1) * 128].reshape(16, 8, 128) for dh in range(3)]
            cols.append(g[1] + shift_h(g[0], -1) + shift_h(g[2], 1))
        acc = cols[1] + shift_w(cols[0], -1) + shift_w(cols[2], 1)
        outs.append(acc.reshape(128, 128))
    return outs


def tm_of(m, j):
    b, xx = j // 8, j % 8 // 2
    return (xx + b * (3 - 2 * xx)) * 8 + 4 * m + 2 * b + j % 2


def kernel(
    clips, k_hbm, cot, act, grad, kg,
    X0, X1, X2, G2, G1, G0, BK, S1, S0, SX, WfA, WfB, WbA, WbB, KX, AG,
    TT, PX, GL, RS, RL, TT2, PX2, GL2, RS2, RL2,
    SS, ownr, x0r, g2r, kr, kxr, acr, grr, pxr, glr, rsr, px2r, gl2r, rs2r, kgr, chr, azr, axr, az2r, ax2r,
):
    s = lax.axis_index("section")
    t = lax.axis_index("tm")
    y = s // 2
    c = s % 2
    x = t // 8
    z = t % 8
    m = z // 4
    b = z % 4 // 2
    j = 8 * b + 2 * (x + b * (3 - 2 * x)) + z % 2
    q = t // 2
    e = t % 2
    first = c == 0
    second = c == 1
    drains = []
    both = jnp.logical_and

    def remote(src, dst, recv, dev, idx):
        return pltpu.make_async_remote_copy(
            src_ref=src, dst_ref=dst, send_sem=SS.at[idx], recv_sem=recv, device_id=dev, device_id_type=MESH
        )

    def send(src, dst, recv, dev, cond=None):
        idx = len(drains)
        make = lambda: remote(src, dst, recv, dev, idx)
        if cond is None:
            make().start()
        else:
            pl.when(cond)(lambda: make().start())
        drains.append((cond, make))

    def send_or_copy(src, dst, recv, dev, cond, own):
        send(src, dst, recv, dev, jnp.logical_and(cond, jnp.logical_not(own)))

        @pl.when(jnp.logical_and(cond, own))
        def _():
            pltpu.make_async_copy(src, dst, recv).start()

    def arrive(dst, recv):
        pltpu.make_async_remote_copy(
            src_ref=dst, dst_ref=dst, send_sem=SS.at[0], recv_sem=recv,
            device_id=(s - c + (1 - c), t), device_id_type=MESH,
        ).wait_recv()

    def arrive_if(cond, dst, recv):
        pl.when(cond)(lambda: arrive(dst, recv))

    def tap_block(ref, tap):
        dt, n = tap // 9, tap % 9
        return ref.at[dt * 128 : (dt + 1) * 128, n * 128 : (n + 1) * 128]

    entry = pltpu.get_barrier_semaphore()
    expected = []

    def greet(cond, dev):
        pl.when(cond)(lambda: pl.semaphore_signal(entry, inc=1, device_id=dev, device_id_type=MESH))

    def expect(cond):
        expected.append(cond.astype(jnp.int32))

    inside = lambda v, top: both(v >= 0, v <= top)
    for k in range(-4, 4):
        at = 2 * j + k
        greet(both(both(second, y == 0), both(inside(at, 31), at != t)), (1, at))
    for dj in (2, 1, 0, -1):
        for mm in range(2):
            ok = both(both(second, y == 0), inside(q + dj, 15))
            expect(both(ok, tm_of(mm, q + dj) != t))
    for dj in (2, 1, 0, -1):
        greet(both(both(second, y > 0), inside(j - dj, 15)), (s - 2, tm_of(m, j - dj)))
        expect(both(both(second, y < PLANES - 1), inside(j + dj, 15)))
    for dj in (-2, -1, 0):
        greet(both(both(second, y < PLANES - 1), inside(j - dj, 15)), (s + 2, tm_of(m, j - dj)))
        expect(both(both(second, y > 0), inside(j + dj, 15)))
    for k in range(6):
        at = 2 * j + k
        greet(both(both(second, y == PLANES - 1), at <= 31), (2 * PLANES - 2, at))
    for dj in (0, -1, -2):
        for mm in range(2):
            expect(both(both(first, y == PLANES - 1), inside(q + dj, 15)))
    always = s >= 0
    for d in range(4):
        greet(first, (s + 1, (x + d) % 4 * 8 + z))
        expect(second)
    greet(second, (s - 1, t))
    expect(first)
    greet(both(first, y > 0), (s - 1, t))
    expect(both(second, y < PLANES - 1))
    greet(both(second, y < PLANES - 1), (s + 1, t))
    expect(both(first, y > 0))
    for d in range(1, 4):
        greet(always, (s, (x + d) % 4 * 8 + z))
        expect(always)
    for d in range(1, 8):
        greet(always, (s, x * 8 + (z + d) % 8))
        expect(always)
    for mm in range(2):
        at = tm_of(mm, q)
        greet(jnp.logical_or(first, at != t), (2 * y + 1, at))
    for k in range(2):
        expect(second)
        expect(both(second, 2 * j + k != t))
    @pl.when(second)
    def _():
        for tap in range(27):
            pltpu.make_async_copy(k_hbm.at[tap], tap_block(WfB, tap), ownr).start()

    pl.semaphore_wait(entry, sum(expected))

    for dj in (2, 1, 0, -1):
        for mm in range(2):
            there = q + dj
            ok = both(both(second, y == 0), both(there >= 0, there <= 15))
            to = tm_of(mm, there)
            send_or_copy(
                clips.at[mm], X0.at[(2 - dj) * 2 + e], x0r.at[2 - dj], (1, to), ok, to == t
            )
    idx = len(drains)
    all_taps = lambda: remote(k_hbm, k_hbm, kr, (s + 1, t), idx)
    drains.append((first, all_taps))

    @pl.when(first)
    def _():
        for tap in range(27):
            remote(k_hbm.at[tap], tap_block(WfA, tap), kr, (s + 1, t), idx).start()

    for dj in (0, -1, -2):
        for mm in range(2):
            there = q + dj
            ok = both(both(first, y == PLANES - 1), both(there >= 0, there <= 15))
            send(cot.at[mm], G2.at[-2 * dj + e], g2r.at[-dj], (2 * PLANES - 1, tm_of(mm, there)), ok)

    def bwd_weight(dst, src):
        for tap in range(27):
            tap_block(dst, tap)[...] = tap_block(src, 26 - tap)[...].astype(F32).T.astype(BF16)

    def frame_silu(ref, k):
        return silu(ref[k].astype(F32)).astype(BF16)

    def build_patches(ref, TT):
        def one(k, carry):
            v = frame_silu(ref, k).astype(F32).reshape(16, 8, 128)
            for dw in range(3):
                vw = v if dw == 1 else shift_w(v, dw - 1)
                for dh in range(3):
                    vh = vw if dh == 1 else shift_h(vw, dh - 1)
                    TT[k, dh * 3 + dw] = vh.reshape(128, 128).T.astype(BF16)
            return carry

        lax.fori_loop(0, 4, one, 0)

    def take(k):
        for at in (k, k + 1):
            SX[at] = frame_silu(X0, at)

    def block_a(lo, hi):
        out = conv([SX[k] for k in range(lo, hi + 2)], WfA)
        for k in range(lo, hi):
            X1[k] = (X0[k + 2].astype(F32) + out[k - lo]).astype(BF16)

    def block_b():
        out = conv([frame_silu(X1, k) for k in range(4)], WfB)
        for k in range(2):
            X2[k] = (X1[k + 2].astype(F32) + out[k]).astype(BF16)

    def back_a(k):
        return conv([G2[at] for at in range(k, k + 4)], WbB)

    def grad_a(k, back):
        G1[k] = (G2[k].astype(F32) + back * S1[k]).astype(BF16)

    def out_home(src, dst, recv, core, cond):
        for k in range(2):
            dev = (2 * y + core, 2 * j + k)
            if core == 0:
                send(src.at[k], dst.at[m], recv.at[m], dev, cond)
            else:
                send_or_copy(src.at[k], dst.at[m], recv.at[m], dev, cond, 2 * j + k == t)

    @pl.when(second)
    def _():
        zero2 = jnp.zeros((2, 128, 128), BF16)

        @pl.when(j < 2)
        def _():
            X0[0:2] = zero2

        @pl.when(j < 1)
        def _():
            X0[2:4] = zero2

        @pl.when(j > 14)
        def _():
            X0[6:8] = zero2
            G2[2:4] = zero2

        @pl.when(j > 13)
        def _():
            G2[4:6] = zero2

        pltpu.make_async_copy(WfB, WfB, ownr).wait()
        arrive(WfA, kr)

        @pl.when(y > 0)
        def _():
            bwd_weight(WbB, WfB)
            bwd_weight(WbA, WfA)

        @pl.when(y == PLANES - 1)
        def _():
            arrive(G2.at[0:2], g2r.at[0])
            arrive_if(j <= 14, G2.at[2:4], g2r.at[1])
            arrive_if(j <= 13, G2.at[4:6], g2r.at[2])
            BK[0], BK[1] = back_a(0)
            BK[2], BK[3] = back_a(2)

        arrive_if(j >= 1, X0.at[2:4], x0r.at[1])
        take(2)

        @pl.when(y < PLANES - 1)
        def _():
            arrive_if(j >= 2, X0.at[0:2], x0r.at[0])
            take(0)
            block_a(0, 2)

        arrive(X0.at[4:6], x0r.at[2])
        take(4)
        block_a(2, 4)

        @pl.when(y < PLANES - 1)
        def _():
            block_b()

        @pl.when(y == PLANES - 1)
        def _():
            arrive_if(j <= 14, X0.at[6:8], x0r.at[3])
            take(6)
            block_a(4, 6)

    forward = both(second, y < PLANES - 1)
    fast = []

    def flush():
        while fast:
            cond, make = fast.pop()
            pl.when(cond)(lambda make=make: make().wait_send())

    def send_fast(src, dst, recv, dev, cond):
        send(src, dst, recv, dev, cond)
        fast.append(drains[-1])
        drains[-1] = None

    odd = j % 2 == 1
    even = j % 2 == 0
    for dj, when in ((1, odd), (2, None), (1, even), (0, None), (-1, y == PLANES - 2), (-1, y < PLANES - 2)):
        there = j + dj
        ok = both(forward, inside(there, 15))
        if when is not None:
            ok = both(ok, when)
        if len(fast) == 5:
            flush()
        send_fast(X2, X0.at[(2 - dj) * 2 : (2 - dj) * 2 + 2], x0r.at[2 - dj], (s + 2, tm_of(m, there)), ok)

    top = both(second, y == PLANES - 1)

    @pl.when(both(second, y == 0))
    def _():
        bwd_weight(WbB, WfB)
        bwd_weight(WbA, WfA)

    @pl.when(both(second, y < PLANES - 1))
    def _():
        arrive_if(j <= 14, X0.at[6:8], x0r.at[3])
        take(6)
        block_a(4, 6)

    flush()
    send(X1.at[0:4], KX, kxr, (s + 1, t), forward)

    def swap_patches(cond, TT, PX, pxr):
        for d in range(4):
            other = (x + d) % 4
            src = TT.at[:, :, pl.ds(pl.multiple_of(32 * other, 32), 32), :]
            if d == 0:
                pl.when(cond)(lambda: pltpu.make_async_copy(src, PX.at[x], pxr.at[0]).start())
            else:
                send(src, PX.at[x], pxr.at[d], (s, other * 8 + z), cond)

    @pl.when(forward)
    def _():
        build_patches(X0.at[2:6], TT)

    swap_patches(forward, TT, PX, pxr)
    out_home(X1.at[2:4], act, acr, 0, forward)
    out_home(X2, act, acr, 1, forward)

    @pl.when(second)
    def _():
        for k in range(4):
            S1[k] = silu_slope(X1[k + 2].astype(F32))
        for k in range(2):
            S0[k] = silu_slope(X0[k + 4].astype(F32))

        @pl.when(y < PLANES - 1)
        def _():
            arrive_if(j <= 14, G2.at[2:4], g2r.at[1])
            arrive_if(j <= 13, G2.at[4:6], g2r.at[2])
            for k, back in zip((2, 3), back_a(2)):
                grad_a(k, back)
            arrive(G2.at[0:2], g2r.at[0])
            for k, back in zip((0, 1), back_a(0)):
                grad_a(k, back)

        @pl.when(y == PLANES - 1)
        def _():
            for k in range(4):
                grad_a(k, BK[k])

    def gather(src, GL, glr, cond):
        for d in (2, 1, 3):
            other = (x + d) % 4
            send(src, GL.at[x], glr.at[d], (s, other * 8 + z), cond)
        pl.when(cond)(lambda: pltpu.make_async_copy(src, GL.at[x], glr.at[0]).start())

    gather(G1.at[0:2], GL, glr, both(second, y == 0))

    @pl.when(second)
    def _():
        out = conv([G1[k] for k in range(4)], WbA)
        for k in range(2):
            G0[k] = (G1[k].astype(F32) + out[k] * S0[k]).astype(BF16)

    for dj, when in ((-1, even), (-2, None), (-1, odd), (0, None)):
        there = j + dj
        ok = both(both(second, y > 0), there >= 0)
        if when is not None:
            ok = both(ok, when)
        send_fast(G0, G2.at[-2 * dj : -2 * dj + 2], g2r.at[-dj], (s - 2, tm_of(m, there)), ok)
    flush()
    behind = both(second, y > 0)
    for d in (2, 1, 3, 0):
        other = (x + d) % 4
        send(G0, GL.at[x], glr.at[d], (s - 1, other * 8 + z), behind)
    gather(G1.at[0:2], GL, glr, behind)
    gather(G2.at[0:2], GL2, gl2r, top)
    out_home(G0, grad, grr, 0, second)
    out_home(G1, grad, grr, 1, second)

    @pl.when(top)
    def _():
        arrive_if(j >= 2, X0.at[0:2], x0r.at[0])
        take(0)
        block_a(0, 2)
        block_b()
        build_patches(X0.at[2:6], TT)
        build_patches(X1, TT2)

    out_home(X1.at[2:4], act, acr, 0, top)
    out_home(X2, act, acr, 1, top)
    swap_patches(top, TT2, PX2, px2r)

    lower = both(first, y > 0)

    @pl.when(lower)
    def _():
        arrive(KX, kxr)
        build_patches(KX, TT)

    swap_patches(jnp.logical_or(lower, top), TT, PX, pxr)

    def chunk(k):
        return pl.ds(pl.multiple_of(k * ROWS, 16), ROWS)

    def reduce_terms(cond, PX, GL, RS, RL, pxr, glr, rsr, out):
        @pl.when(cond)
        def _():
            for d in range(4):
                source = (x + 4 - d) % 4
                arrive(PX.at[source], pxr.at[d])
                arrive(GL.at[source], glr.at[d])
            for dt in range(3):
                total = None
                for p in range(4):
                    left = jnp.concatenate(
                        [PX[p, dt].reshape(288, 128), PX[p, dt + 1].reshape(288, 128)], axis=1
                    )
                    term = jnp.dot(left, GL[p].reshape(256, 128), preferred_element_type=F32)
                    total = term if total is None else total + term
                RS[dt * 288 : (dt + 1) * 288, :] = total.astype(BF16)
            RS[864:896, :] = jnp.zeros((32, 128), BF16)

        for d in (4, 3, 5, 2, 6, 1, 7):
            other = (z + d) % 8
            send(RS.at[chunk(other)], RL.at[z], rsr.at[d], (s, x * 8 + other), cond)

        @pl.when(cond)
        def _():
            total = RS[chunk(z), :].astype(F32)
            for d in range(1, 8):
                source = (z + 8 - d) % 8
                arrive(RL.at[source], rsr.at[d])
                total = total + RL[source].astype(F32)
            out[...] = total.astype(BF16)

    right, left, far = (x + 1) % 4, (x + 3) % 4, (x + 2) % 4
    order = (0, 1, 7, 2, 6, 3, 5, 4)

    def piece(ref, row, d):
        return ref.at[row, chunk((z + 8 - d) % 8)]

    def pass_on(buf, row, d, recv, dev):
        send(piece(buf, row, d), piece(buf, row, d), recv, dev, second)

    def hand_over(row, d):
        send(piece(AG, row, d), piece(kg, row, d), kgr, (s - 1, t), second)

    def along_z(buf, azr):
        for d in (4, 3, 5, 2, 6, 1, 7):
            pass_on(buf, x, 0, azr.at[d], (s, x * 8 + (z + d) % 8))

    def along_x(buf, azr, axr):
        for d in order:
            if d:
                arrive_if(second, piece(buf, x, d), azr.at[d])
            pass_on(buf, x, d, axr.at[0, d], (s, right * 8 + z))
            pass_on(buf, x, d, axr.at[1, d], (s, left * 8 + z))

    def further_x(buf, axr):
        for at, d in enumerate(order):
            arrive_if(second, piece(buf, left, d), axr.at[0, d])
            arrive_if(second, piece(buf, right, d), axr.at[1, d])
            if at % 2:
                pass_on(buf, left, d, axr.at[2, d], (s, right * 8 + z))
            else:
                pass_on(buf, right, d, axr.at[2, d], (s, left * 8 + z))

    working = s > 0
    mine = kg.at[x, chunk(z)]
    own_sum = AG.at[x, chunk(z)]
    reduce_terms(working, PX, GL, RS, RL, pxr, glr, rsr, own_sum)
    send(own_sum, mine, chr, (s - 1, t), lower)
    along_z(AG, azr)
    reduce_terms(top, PX2, GL2, RS2, RL2, px2r, gl2r, rs2r, mine)
    arrive_if(forward, mine, chr)
    along_z(kg, az2r)
    along_x(AG, azr, axr)
    along_x(kg, az2r, ax2r)
    further_x(AG, axr)
    further_x(kg, ax2r)
    for row in (x, left, right):
        for d in order:
            hand_over(row, d)
    for d in order:
        arrive_if(second, piece(AG, far, d), axr.at[2, d])
        hand_over(far, d)
    for d in order:
        arrive_if(second, piece(kg, far, d), ax2r.at[2, d])
    arrive_if(first, kg, kgr)
    for mm in range(2):
        arrive(act.at[mm], acr.at[mm])
        arrive(grad.at[mm], grr.at[mm])
    for cond, make in filter(None, drains):
        if cond is None:
            make().wait_send()
        else:
            pl.when(cond)(lambda make=make: make().wait_send())


def body(clips, kernels, cotangent):
    micro, frames, height, width, chan = clips.shape
    vmem = pl.BlockSpec(memory_space=pltpu.VMEM)
    frame = lambda n: pltpu.VMEM((n, 128, 128), BF16)
    weight = pltpu.VMEM((384, 1152), BF16)
    dma = pltpu.SemaphoreType.DMA
    terms = (
        pltpu.VMEM((4, 9, 128, 128), BF16),
        pltpu.VMEM((4, 4, 9, 32, 128), BF16),
        pltpu.VMEM((4, 2, 128, 128), BF16),
        pltpu.VMEM((8 * ROWS, 128), BF16),
        pltpu.VMEM((8, ROWS, 128), BF16),
    )
    act, grad, kg = pl.pallas_call(
        kernel,
        out_shape=(
            jax.ShapeDtypeStruct((2, 128, 128), BF16),
            jax.ShapeDtypeStruct((2, 128, 128), BF16),
            jax.ShapeDtypeStruct((4, 8 * ROWS, 128), BF16),
        ),
        in_specs=[pl.BlockSpec(memory_space=pl.ANY)] * 3,
        out_specs=(vmem,) * 3,
        scratch_shapes=[
            frame(8), frame(6), frame(2), frame(6), frame(4), frame(2),
            pltpu.VMEM((4, 128, 128), F32),
            pltpu.VMEM((4, 128, 128), F32),
            pltpu.VMEM((2, 128, 128), F32),
            frame(8), weight, weight, weight, weight, frame(4), pltpu.VMEM((4, 8 * ROWS, 128), BF16),
            *terms, *terms,
            dma((220,)), dma, dma((4,)), dma((3,)), dma, dma, dma((2,)), dma((2,)),
            dma((4,)), dma((4,)), dma((8,)), dma((4,)), dma((4,)), dma((8,)),
            dma, dma, dma((8,)), dma((3, 8)), dma((8,)), dma((3, 8)),
        ],
        compiler_params=pltpu.CompilerParams(
            collective_id=0, has_side_effects=True, vmem_limit_bytes=48 << 20,
        ),
        name="blocks",
    )(
        clips.reshape(2, 128, 128),
        kernels.reshape(27, 128, 128),
        cotangent.reshape(2, 128, 128),
    )
    total = micro * frames * lax.axis_size("tm") * height * width
    norm = 1.0 / jnp.sqrt(jnp.float32(total))
    parts = kg[:, :864].reshape(4, 27, 32, 128).transpose(1, 0, 2, 3).astype(F32) * norm
    return (
        act.reshape(1, micro, 1, height, width, chan),
        grad.reshape(1, micro, 1, height, width, chan),
        parts.reshape(1, 3, 3, 3, chan, chan),
    )


def solution(mesh):
    placed = (
        P(None, "tm", None, None, None),
        P("section", None, None, None, None, None),
        P(None, "tm", None, None, None),
    )
    return jax.shard_map(
        body,
        mesh=mesh,
        in_specs=placed,
        out_specs=(
            P("section", None, "tm", None, None, None),
            P("section", None, "tm", None, None, None),
            P("section", None, None, None, None, None),
        ),
        check_vma=False,
    )
```

```python
import functools

import jax
import jax.numpy as jnp
from jax import lax
from jax.experimental import pallas as pl
from jax.experimental.pallas import tpu as pltpu
from jax.sharding import PartitionSpec as P

MESH = pl.DeviceIdType.MESH
PLANES = 8
CLIP_PLANE = {2: 0, 1: 0, 0: 0, -1: 0}
BF16 = jnp.bfloat16
F32 = jnp.float32


def logistic(v):
    return 0.5 + 0.5 * jnp.tanh(0.5 * v)


def silu(v):
    return v * logistic(v)


def silu_slope(v):
    sig = logistic(v)
    return sig * (1.0 + v * (1.0 - sig))


def shift_w(a, d):
    r = pltpu.roll(a, (-d) % 8, 1)
    w = lax.broadcasted_iota(jnp.int32, a.shape, 1)
    return jnp.where(w < 7, r, 0.0) if d == 1 else jnp.where(w > 0, r, 0.0)


def shift_h(a, d):
    z = jnp.zeros((1,) + a.shape[1:], a.dtype)
    return jnp.concatenate([a[1:], z], axis=0) if d == 1 else jnp.concatenate([z, a[:-1]], axis=0)


def conv(frames, weight):
    count = len(frames) - 2
    rows = [jnp.concatenate(frames[f : f + 3], axis=1) for f in range(count)]
    left = jnp.concatenate(rows, axis=0) if count > 1 else rows[0]
    full = jnp.dot(left, weight[...], preferred_element_type=F32)
    outs = []
    for f in range(count):
        part = full[f * 128 : (f + 1) * 128]
        cols = []
        for dw in range(3):
            g = [part[:, (dh * 3 + dw) * 128 : (dh * 3 + dw + 1) * 128].reshape(16, 8, 128) for dh in range(3)]
            cols.append(g[1] + shift_h(g[0], -1) + shift_h(g[2], 1))
        acc = cols[1] + shift_w(cols[0], -1) + shift_w(cols[2], 1)
        outs.append(acc.reshape(128, 128))
    return outs


def tm_of(m, j):
    b, xx = j // 8, j % 8 // 2
    return (xx + b * (3 - 2 * xx)) * 8 + 4 * m + 2 * b + j % 2


def kernel(
    clips_hbm, k_hbm, cot, act, grad, kg,
    X0, X1, X2, G2, G1, G0, BK, S1, S0, SX, clips, WfA, WfB, WbA, WbB, KX, AG, CH,
    TT, PX, GL, RS, RL, TT2, PX2, GL2, RS2, RL2,
    SS, ownr, clr, x0r, g2r, kr, kxr, acr, grr, pxr, glr, rsr, px2r, gl2r, rs2r, kgr, chr, evr, azr, axr, az2r, ax2r,
):
    s = lax.axis_index("section")
    t = lax.axis_index("tm")
    y = s // 2
    c = s % 2
    x = t // 8
    z = t % 8
    m = z // 4
    b = z % 4 // 2
    j = 8 * b + 2 * (x + b * (3 - 2 * x)) + z % 2
    q = t // 2
    e = t % 2
    first = c == 0
    second = c == 1
    drains = []
    both = jnp.logical_and

    def remote(src, dst, recv, dev, idx):
        return pltpu.make_async_remote_copy(
            src_ref=src, dst_ref=dst, send_sem=SS.at[idx], recv_sem=recv, device_id=dev, device_id_type=MESH
        )

    def send(src, dst, recv, dev, cond=None):
        idx = len(drains)
        make = lambda: remote(src, dst, recv, dev, idx)
        if cond is None:
            make().start()
        else:
            pl.when(cond)(lambda: make().start())
        drains.append((cond, make))

    def send_or_copy(src, dst, recv, dev, cond, own):
        send(src, dst, recv, dev, jnp.logical_and(cond, jnp.logical_not(own)))

        @pl.when(jnp.logical_and(cond, own))
        def _():
            pltpu.make_async_copy(src, dst, recv).start()

    def arrive(dst, recv):
        pltpu.make_async_remote_copy(
            src_ref=dst, dst_ref=dst, send_sem=SS.at[0], recv_sem=recv,
            device_id=(s - c + (1 - c), t), device_id_type=MESH,
        ).wait_recv()

    def arrive_if(cond, dst, recv):
        pl.when(cond)(lambda: arrive(dst, recv))

    def tap_block(ref, tap):
        dt, n = tap // 9, tap % 9
        return ref.at[dt * 128 : (dt + 1) * 128, n * 128 : (n + 1) * 128]

    base = both(second, y == 0)
    pl.when(base)(lambda: pltpu.make_async_copy(clips_hbm, clips, clr).start())
    entry = pltpu.get_barrier_semaphore()
    expected = []

    def greet(cond, dev):
        pl.when(cond)(lambda: pl.semaphore_signal(entry, inc=1, device_id=dev, device_id_type=MESH))

    def expect(cond):
        expected.append(cond.astype(jnp.int32))

    always = s >= 0
    for d in (4, 3, 5, 2, 6, 1, 7):
        greet(always, (s, x * 8 + (z + d) % 8))
        expect(always)
    inside = lambda v, top: both(v >= 0, v <= top)
    for k in range(-4, 4):
        at = 2 * j + k
        plane = CLIP_PLANE[-(k // 2)]
        away = at != t if plane == 0 else always
        greet(both(both(second, y == 0), both(inside(at, 31), away)), (2 * plane + 1, at))
    for dj in (2, 1, 0, -1):
        for mm in range(2):
            away = tm_of(mm, q + dj) != t if CLIP_PLANE[dj] == 0 else always
            expect(both(both(second, y == CLIP_PLANE[dj]), both(inside(q + dj, 15), away)))
    for dj in (2, 1, 0, -1):
        greet(both(both(second, y > 0), inside(j - dj, 15)), (s - 2, tm_of(m, j - dj)))
        expect(both(both(second, y < PLANES - 1), inside(j + dj, 15)))
    for dj in (-2, -1, 0):
        greet(both(both(second, y < PLANES - 1), inside(j - dj, 15)), (s + 2, tm_of(m, j - dj)))
        expect(both(both(second, y > 0), inside(j + dj, 15)))
    for k in range(6):
        at = 2 * j + k
        greet(both(both(second, y == PLANES - 1), at <= 31), (2 * PLANES - 2, at))
    for dj in (0, -1, -2):
        for mm in range(2):
            expect(both(both(first, y == PLANES - 1), inside(q + dj, 15)))
    for d in range(4):
        greet(first, (s + 1, (x + d) % 4 * 8 + z))
        expect(second)
    greet(second, (s - 1, t))
    expect(first)
    for d in range(1, 4):
        greet(always, (s, (x + d) % 4 * 8 + z))
        expect(always)
    for mm in range(2):
        at = tm_of(mm, q)
        greet(jnp.logical_or(first, at != t), (2 * y + 1, at))
    for k in range(2):
        expect(second)
        expect(both(second, 2 * j + k != t))
    @pl.when(second)
    def _():
        for tap in range(27):
            pltpu.make_async_copy(k_hbm.at[tap], tap_block(WfB, tap), ownr).start()

    pl.semaphore_wait(entry, sum(expected))

    pl.when(base)(lambda: pltpu.make_async_copy(clips_hbm, clips, clr).wait())

    for dj in (2, 1, 0, -1):
        for mm in range(2):
            there = q + dj
            ok = both(both(second, y == CLIP_PLANE[dj]), inside(there, 15))
            to = tm_of(mm, there)
            slot = (2 - dj) * 2 + e
            if CLIP_PLANE[dj] == 0:
                send_or_copy(clips.at[mm], X0.at[slot], x0r.at[2 - dj], (1, to), ok, to == t)
            else:
                send(clips.at[mm], X0.at[slot], x0r.at[2 - dj], (1, to), ok)
    idx = len(drains)
    all_taps = lambda: remote(k_hbm, k_hbm, kr, (s + 1, t), idx)
    drains.append((first, all_taps))

    @pl.when(first)
    def _():
        for tap in range(27):
            remote(k_hbm.at[tap], tap_block(WfA, tap), kr, (s + 1, t), idx).start()

    for dj in (0, -1, -2):
        for mm in range(2):
            there = q + dj
            ok = both(both(first, y == PLANES - 1), both(there >= 0, there <= 15))
            send(cot.at[mm], G2.at[-2 * dj + e], g2r.at[-dj], (2 * PLANES - 1, tm_of(mm, there)), ok)

    def bwd_weight(dst, src):
        for tap in range(27):
            tap_block(dst, tap)[...] = tap_block(src, 26 - tap)[...].astype(F32).T.astype(BF16)

    def frame_silu(ref, k):
        return silu(ref[k].astype(F32)).astype(BF16)

    def build_patches(ref, TT):
        def one(k, carry):
            v = frame_silu(ref, k).astype(F32).reshape(16, 8, 128)
            for dw in range(3):
                vw = v if dw == 1 else shift_w(v, dw - 1)
                for dh in range(3):
                    vh = vw if dh == 1 else shift_h(vw, dh - 1)
                    TT[k, dh * 3 + dw] = vh.reshape(128, 128).T.astype(BF16)
            return carry

        lax.fori_loop(0, 4, one, 0)

    def take(k):
        for at in (k, k + 1):
            SX[at] = frame_silu(X0, at)

    def block_a(lo, hi):
        out = conv([SX[k] for k in range(lo, hi + 2)], WfA)
        for k in range(lo, hi):
            X1[k] = (X0[k + 2].astype(F32) + out[k - lo]).astype(BF16)

    def block_b():
        out = conv([frame_silu(X1, k) for k in range(4)], WfB)
        for k in range(2):
            X2[k] = (X1[k + 2].astype(F32) + out[k]).astype(BF16)

    def back_a(k):
        return conv([G2[at] for at in range(k, k + 4)], WbB)

    def grad_a(k, back):
        G1[k] = (G2[k].astype(F32) + back * S1[k]).astype(BF16)

    def out_home(src, dst, recv, core, cond):
        for k in range(2):
            dev = (2 * y + core, 2 * j + k)
            if core == 0:
                send(src.at[k], dst.at[m], recv.at[m], dev, cond)
            else:
                send_or_copy(src.at[k], dst.at[m], recv.at[m], dev, cond, 2 * j + k == t)

    @pl.when(second)
    def _():
        zero2 = jnp.zeros((2, 128, 128), BF16)

        @pl.when(j < 2)
        def _():
            X0[0:2] = zero2

        @pl.when(j < 1)
        def _():
            X0[2:4] = zero2

        @pl.when(j > 14)
        def _():
            X0[6:8] = zero2
            G2[2:4] = zero2

        @pl.when(j > 13)
        def _():
            G2[4:6] = zero2

        pltpu.make_async_copy(WfB, WfB, ownr).wait()
        arrive(WfA, kr)

        @pl.when(y > 2)
        def _():
            bwd_weight(WbB, WfB)
            bwd_weight(WbA, WfA)

        @pl.when(y == PLANES - 1)
        def _():
            arrive(G2.at[0:2], g2r.at[0])
            arrive_if(j <= 14, G2.at[2:4], g2r.at[1])
            arrive_if(j <= 13, G2.at[4:6], g2r.at[2])
            BK[0], BK[1] = back_a(0)
            BK[2], BK[3] = back_a(2)

        arrive_if(j >= 1, X0.at[2:4], x0r.at[1])
        take(2)

        @pl.when(y < PLANES - 1)
        def _():
            arrive_if(j >= 2, X0.at[0:2], x0r.at[0])
            take(0)
            block_a(0, 2)

        arrive(X0.at[4:6], x0r.at[2])
        take(4)
        block_a(2, 4)

        @pl.when(y < PLANES - 1)
        def _():
            block_b()

        @pl.when(y == PLANES - 1)
        def _():
            arrive_if(j <= 14, X0.at[6:8], x0r.at[3])
            take(6)
            block_a(4, 6)

    forward = both(second, y < PLANES - 1)
    fast = []

    def flush():
        while fast:
            cond, make = fast.pop()
            pl.when(cond)(lambda make=make: make().wait_send())

    def send_fast(src, dst, recv, dev, cond):
        send(src, dst, recv, dev, cond)
        fast.append(drains[-1])
        drains[-1] = None

    odd = j % 2 == 1
    even = j % 2 == 0
    for dj, when in ((1, odd), (2, None), (1, even), (0, None), (-1, y == PLANES - 2), (-1, y < PLANES - 2)):
        there = j + dj
        ok = both(forward, inside(there, 15))
        if when is not None:
            ok = both(ok, when)
        if len(fast) == 5:
            flush()
        send_fast(X2, X0.at[(2 - dj) * 2 : (2 - dj) * 2 + 2], x0r.at[2 - dj], (s + 2, tm_of(m, there)), ok)

    top = both(second, y == PLANES - 1)

    @pl.when(both(second, y <= 2))
    def _():
        bwd_weight(WbB, WfB)
        bwd_weight(WbA, WfA)

    @pl.when(both(second, y < PLANES - 1))
    def _():
        arrive_if(j <= 14, X0.at[6:8], x0r.at[3])
        take(6)
        block_a(4, 6)

    flush()
    behind = both(second, y > 0)
    lower = both(first, y > 0)
    ground = both(second, y == 0)
    send(X1.at[0:4], KX, kxr, (s + 2, t), forward)
    send(X0.at[2:6], KX, kxr, (s - 1, t), behind)

    def swap_patches(cond, TT, PX, pxr):
        for d in range(4):
            other = (x + d) % 4
            src = TT.at[:, :, pl.ds(pl.multiple_of(32 * other, 32), 32), :]
            if d == 0:
                pl.when(cond)(lambda: pltpu.make_async_copy(src, PX.at[x], pxr.at[0]).start())
            else:
                send(src, PX.at[x], pxr.at[d], (s, other * 8 + z), cond)

    @pl.when(ground)
    def _():
        build_patches(X0.at[2:6], TT)

    @pl.when(both(forward, y > 0))
    def _():
        arrive(KX, kxr)
        build_patches(KX, TT)

    swap_patches(forward, TT, PX, pxr)
    out_home(X1.at[2:4], act, acr, 0, forward)
    out_home(X2, act, acr, 1, forward)

    @pl.when(second)
    def _():
        for k in range(4):
            S1[k] = silu_slope(X1[k + 2].astype(F32))
        for k in range(2):
            S0[k] = silu_slope(X0[k + 4].astype(F32))

        @pl.when(y < PLANES - 1)
        def _():
            arrive_if(j <= 14, G2.at[2:4], g2r.at[1])
            arrive_if(j <= 13, G2.at[4:6], g2r.at[2])
            for k, back in zip((2, 3), back_a(2)):
                grad_a(k, back)
            arrive(G2.at[0:2], g2r.at[0])
            for k, back in zip((0, 1), back_a(0)):
                grad_a(k, back)

        @pl.when(y == PLANES - 1)
        def _():
            for k in range(4):
                grad_a(k, BK[k])

    def gather(src, GL, glr, cond):
        for d in (2, 1, 3):
            other = (x + d) % 4
            send(src, GL.at[x], glr.at[d], (s, other * 8 + z), cond)
        pl.when(cond)(lambda: pltpu.make_async_copy(src, GL.at[x], glr.at[0]).start())

    gather(G1.at[0:2], GL, glr, ground)

    @pl.when(second)
    def _():
        out = conv([G1[k] for k in range(4)], WbA)
        for k in range(2):
            G0[k] = (G1[k].astype(F32) + out[k] * S0[k]).astype(BF16)

    for dj, when in ((-1, even), (-2, None), (-1, odd), (0, None)):
        there = j + dj
        ok = both(both(second, y > 0), there >= 0)
        if when is not None:
            ok = both(ok, when)
        send_fast(G0, G2.at[-2 * dj : -2 * dj + 2], g2r.at[-dj], (s - 2, tm_of(m, there)), ok)
    flush()
    gather(G0, GL, glr, behind)
    for d in (2, 1, 3, 0):
        other = (x + d) % 4
        send(G1.at[0:2], GL.at[x], glr.at[d], (s - 1, other * 8 + z), behind)
    gather(G2.at[0:2], GL2, gl2r, top)
    out_home(G0, grad, grr, 0, behind)
    out_home(G1, grad, grr, 1, behind)

    @pl.when(top)
    def _():
        arrive_if(j >= 2, X0.at[0:2], x0r.at[0])
        take(0)
        block_a(0, 2)
        block_b()
        build_patches(X1, TT2)

    out_home(X1.at[2:4], act, acr, 0, top)
    out_home(X2, act, acr, 1, top)
    swap_patches(top, TT2, PX2, px2r)

    @pl.when(jnp.logical_or(lower, top))
    def _():
        arrive(KX, kxr)
        build_patches(KX, TT)

    swap_patches(jnp.logical_or(lower, top), TT, PX, pxr)

    def taps_of(k):
        return pl.ds(7 * (k % 4), 7)

    def reduce_terms(cond, PX, GL, RS, RL, pxr, glr, rsr, out, between=lambda: None):
        @pl.when(cond)
        def _():
            for d in range(4):
                source = (x + 4 - d) % 4
                arrive(PX.at[source], pxr.at[d])
                arrive(GL.at[source], glr.at[d])
            for dt in range(3):
                total = None
                for p in range(4):
                    left = jnp.concatenate(
                        [PX[p, dt].reshape(288, 128), PX[p, dt + 1].reshape(288, 128)], axis=1
                    )
                    term = jnp.dot(left, GL[p].reshape(256, 128), preferred_element_type=F32)
                    total = term if total is None else total + term
                RS[dt * 9 : (dt + 1) * 9] = total.astype(BF16).reshape(9, 2, 16, 128)
            RS[27] = jnp.zeros((2, 16, 128), BF16)

        for d in (4, 3, 5, 2, 6, 1, 7):
            other = (z + d) % 8
            send(RS.at[taps_of(other), other // 4], RL.at[z], rsr.at[d], (s, x * 8 + other), cond)
        between()

        @pl.when(cond)
        def _():
            total = RS[taps_of(z), z // 4].astype(F32)
            for d in range(1, 8):
                source = (z + 8 - d) % 8
                arrive(RL.at[source], rsr.at[d])
                total = total + RL[source].astype(F32)
            out[...] = total.astype(BF16)

    right, left, far = (x + 1) % 4, (x + 3) % 4, (x + 2) % 4
    order = (0, 1, 7, 2, 6, 3, 5, 4)

    def piece(ref, row, d):
        k = (z + 8 - d) % 8
        return ref.at[taps_of(k), 2 * row + k // 4]

    def pass_on(buf, row, d, recv, dev):
        send(piece(buf, row, d), piece(buf, row, d), recv, dev, second)

    def hand_over(row, d):
        send(piece(AG, row, d), piece(kg, row, d), kgr, (s - 1, t), second)

    def along_z(buf, azr):
        for d in (4, 3, 5, 2, 6, 1, 7):
            pass_on(buf, x, 0, azr.at[d], (s, x * 8 + (z + d) % 8))

    def along_x(buf, azr, axr):
        for d in order:
            if d:
                arrive_if(second, piece(buf, x, d), azr.at[d])
            pass_on(buf, x, d, axr.at[0, d], (s, right * 8 + z))
            pass_on(buf, x, d, axr.at[1, d], (s, left * 8 + z))

    def further_x(buf, axr):
        for at, d in enumerate(order):
            arrive_if(second, piece(buf, left, d), axr.at[0, d])
            arrive_if(second, piece(buf, right, d), axr.at[1, d])
            if at % 2:
                pass_on(buf, left, d, axr.at[2, d], (s, right * 8 + z))
            else:
                pass_on(buf, right, d, axr.at[2, d], (s, left * 8 + z))

    mine = piece(kg, x, 0)
    even_sum = piece(AG, x, 0)
    def last_home():
        out_home(G0, grad, grr, 0, ground)
        out_home(G1, grad, grr, 1, ground)

    reduce_terms(s > 0, PX, GL, RS, RL, pxr, glr, rsr, CH, last_home)
    send(CH, mine, chr, (s - 2, t), behind)
    send(CH, even_sum, evr, (s + 1, t), lower)

    @pl.when(ground)
    def _():
        even_sum[...] = CH[...]

    arrive_if(behind, even_sum, evr)
    along_z(AG, azr)
    reduce_terms(top, PX2, GL2, RS2, RL2, px2r, gl2r, rs2r, mine)
    arrive_if(forward, mine, chr)
    along_z(kg, az2r)
    along_x(AG, azr, axr)
    along_x(kg, az2r, ax2r)
    further_x(AG, axr)
    further_x(kg, ax2r)
    for row in (x, left, right):
        for d in order:
            hand_over(row, d)
    for d in order:
        arrive_if(second, piece(AG, far, d), axr.at[2, d])
        hand_over(far, d)
    for d in order:
        arrive_if(second, piece(kg, far, d), ax2r.at[2, d])
    arrive_if(first, kg, kgr)
    for mm in range(2):
        arrive(act.at[mm], acr.at[mm])
        arrive(grad.at[mm], grr.at[mm])
    for cond, make in filter(None, drains):
        if cond is None:
            make().wait_send()
        else:
            pl.when(cond)(lambda make=make: make().wait_send())


def body(clips, kernels, cotangent):
    micro, frames, height, width, chan = clips.shape
    vmem = pl.BlockSpec(memory_space=pltpu.VMEM)
    frame = lambda n: pltpu.VMEM((n, 128, 128), BF16)
    weight = pltpu.VMEM((384, 1152), BF16)
    dma = pltpu.SemaphoreType.DMA
    terms = (
        pltpu.VMEM((4, 9, 128, 128), BF16),
        pltpu.VMEM((4, 4, 9, 32, 128), BF16),
        pltpu.VMEM((4, 2, 128, 128), BF16),
        pltpu.VMEM((28, 2, 16, 128), BF16),
        pltpu.VMEM((8, 7, 16, 128), BF16),
    )
    act, grad, kg = pl.pallas_call(
        kernel,
        out_shape=(
            jax.ShapeDtypeStruct((2, 128, 128), BF16),
            jax.ShapeDtypeStruct((2, 128, 128), BF16),
            jax.ShapeDtypeStruct((28, 8, 16, 128), BF16),
        ),
        in_specs=[pl.BlockSpec(memory_space=pltpu.HBM)] * 3,
        out_specs=(vmem,) * 3,
        scratch_shapes=[
            frame(8), frame(6), frame(2), frame(6), frame(4), frame(2),
            pltpu.VMEM((4, 128, 128), F32),
            pltpu.VMEM((4, 128, 128), F32),
            pltpu.VMEM((2, 128, 128), F32),
            frame(8), frame(2), weight, weight, weight, weight, frame(4), pltpu.VMEM((28, 8, 16, 128), BF16), pltpu.VMEM((7, 16, 128), BF16),
            *terms, *terms,
            dma((220,)), dma, dma, dma((4,)), dma((3,)), dma, dma, dma((2,)), dma((2,)),
            dma((4,)), dma((4,)), dma((8,)), dma((4,)), dma((4,)), dma((8,)),
            dma, dma, dma, dma((8,)), dma((3, 8)), dma((8,)), dma((3, 8)),
        ],
        compiler_params=pltpu.CompilerParams(
            collective_id=0, has_side_effects=True, vmem_limit_bytes=60 << 20,
        ),
        name="blocks",
    )(
        clips.reshape(2, 128, 128),
        kernels.reshape(27, 128, 128),
        cotangent.reshape(2, 128, 128),
    )
    total = micro * frames * lax.axis_size("tm") * height * width
    norm = 1.0 / jnp.sqrt(jnp.float32(total))
    parts = kg[:27].reshape(27, chan, chan).astype(F32) * norm
    return (
        act.reshape(1, micro, 1, height, width, chan),
        grad.reshape(1, micro, 1, height, width, chan),
        parts.reshape(1, 3, 3, 3, chan, chan),
    )


def solution(mesh):
    placed = (
        P(None, "tm", None, None, None),
        P("section", None, None, None, None, None),
        P(None, "tm", None, None, None),
    )
    return jax.shard_map(
        body,
        mesh=mesh,
        in_specs=placed,
        out_specs=(
            P("section", None, "tm", None, None, None),
            P("section", None, "tm", None, None, None),
            P("section", None, None, None, None, None),
        ),
        check_vma=False,
    )
```

```python
import functools

import jax
import jax.numpy as jnp
from jax import lax
from jax.experimental import pallas as pl
from jax.experimental.pallas import tpu as pltpu
from jax.sharding import PartitionSpec as P

MESH = pl.DeviceIdType.MESH
PLANES = 8
CLIP_PLANE = {2: 0, 1: 0, 0: 0, -1: 0}
BF16 = jnp.bfloat16
F32 = jnp.float32


def logistic(v):
    return 0.5 + 0.5 * jnp.tanh(0.5 * v)


def silu(v):
    return v * logistic(v)


def silu_slope(v):
    sig = logistic(v)
    return sig * (1.0 + v * (1.0 - sig))


def shift_w(a, d):
    r = pltpu.roll(a, (-d) % 8, 1)
    w = lax.broadcasted_iota(jnp.int32, a.shape, 1)
    return jnp.where(w < 7, r, 0.0) if d == 1 else jnp.where(w > 0, r, 0.0)


def shift_h(a, d):
    z = jnp.zeros((1,) + a.shape[1:], a.dtype)
    return jnp.concatenate([a[1:], z], axis=0) if d == 1 else jnp.concatenate([z, a[:-1]], axis=0)


def conv(frames, weight):
    count = len(frames) - 2
    rows = [jnp.concatenate(frames[f : f + 3], axis=1) for f in range(count)]
    left = jnp.concatenate(rows, axis=0) if count > 1 else rows[0]
    full = jnp.dot(left, weight[...], preferred_element_type=F32)
    outs = []
    for f in range(count):
        part = full[f * 128 : (f + 1) * 128]
        cols = []
        for dw in range(3):
            g = [part[:, (dh * 3 + dw) * 128 : (dh * 3 + dw + 1) * 128].reshape(16, 8, 128) for dh in range(3)]
            cols.append(g[1] + shift_h(g[0], -1) + shift_h(g[2], 1))
        acc = cols[1] + shift_w(cols[0], -1) + shift_w(cols[2], 1)
        outs.append(acc.reshape(128, 128))
    return outs


def tm_of(m, j):
    b, xx = j // 8, j % 8 // 2
    return (xx + b * (3 - 2 * xx)) * 8 + 4 * m + 2 * b + j % 2


def kernel(
    clips_hbm, k_hbm, cot, act, grad, kg,
    X0, X1, X2, G2, G1, G0, BK, S1, S0, SX, SB, clips, WfA, WfB, WbA, WbB, KX, AG, CH,
    TT, PX, GL, RS, RL, TT2, PX2, GL2, RS2, RL2,
    SS, ownr, clr, x0r, g2r, kr, kxr, acr, grr, pxr, glr, rsr, px2r, gl2r, rs2r, kgr, chr, evr, azr, axr, az2r, ax2r,
):
    s = lax.axis_index("section")
    t = lax.axis_index("tm")
    y = s // 2
    c = s % 2
    x = t // 8
    z = t % 8
    m = z // 4
    b = z % 4 // 2
    j = 8 * b + 2 * (x + b * (3 - 2 * x)) + z % 2
    q = t // 2
    e = t % 2
    first = c == 0
    second = c == 1
    drains = []
    both = jnp.logical_and

    def remote(src, dst, recv, dev, idx):
        return pltpu.make_async_remote_copy(
            src_ref=src, dst_ref=dst, send_sem=SS.at[idx], recv_sem=recv, device_id=dev, device_id_type=MESH
        )

    def send(src, dst, recv, dev, cond=None):
        idx = len(drains)
        make = lambda: remote(src, dst, recv, dev, idx)
        if cond is None:
            make().start()
        else:
            pl.when(cond)(lambda: make().start())
        drains.append((cond, make))

    def send_or_copy(src, dst, recv, dev, cond, own):
        send(src, dst, recv, dev, jnp.logical_and(cond, jnp.logical_not(own)))

        @pl.when(jnp.logical_and(cond, own))
        def _():
            pltpu.make_async_copy(src, dst, recv).start()

    def arrive(dst, recv):
        pltpu.make_async_remote_copy(
            src_ref=dst, dst_ref=dst, send_sem=SS.at[0], recv_sem=recv,
            device_id=(s - c + (1 - c), t), device_id_type=MESH,
        ).wait_recv()

    def arrive_if(cond, dst, recv):
        pl.when(cond)(lambda: arrive(dst, recv))

    def tap_block(ref, tap):
        dt, n = tap // 9, tap % 9
        return ref.at[dt * 128 : (dt + 1) * 128, n * 128 : (n + 1) * 128]

    base = both(second, y == 0)
    pl.when(base)(lambda: pltpu.make_async_copy(clips_hbm, clips, clr).start())
    entry = pltpu.get_barrier_semaphore()
    expected = []

    def greet(cond, dev):
        pl.when(cond)(lambda: pl.semaphore_signal(entry, inc=1, device_id=dev, device_id_type=MESH))

    def expect(cond):
        expected.append(cond.astype(jnp.int32))

    always = s >= 0
    for d in (4, 3, 5, 2, 6, 1, 7):
        greet(always, (s, x * 8 + (z + d) % 8))
        expect(always)
    inside = lambda v, top: both(v >= 0, v <= top)
    for k in range(-4, 4):
        at = 2 * j + k
        plane = CLIP_PLANE[-(k // 2)]
        away = at != t if plane == 0 else always
        greet(both(both(second, y == 0), both(inside(at, 31), away)), (2 * plane + 1, at))
    for dj in (2, 1, 0, -1):
        for mm in range(2):
            away = tm_of(mm, q + dj) != t if CLIP_PLANE[dj] == 0 else always
            expect(both(both(second, y == CLIP_PLANE[dj]), both(inside(q + dj, 15), away)))
    for dj in (2, 1, 0, -1):
        greet(both(both(second, y > 0), inside(j - dj, 15)), (s - 2, tm_of(m, j - dj)))
        expect(both(both(second, y < PLANES - 1), inside(j + dj, 15)))
    for dj in (-2, -1, 0):
        greet(both(both(second, y < PLANES - 1), inside(j - dj, 15)), (s + 2, tm_of(m, j - dj)))
        expect(both(both(second, y > 0), inside(j + dj, 15)))
    for k in range(6):
        at = 2 * j + k
        greet(both(both(second, y == PLANES - 1), at <= 31), (2 * PLANES - 2, at))
    for dj in (0, -1, -2):
        for mm in range(2):
            expect(both(both(first, y == PLANES - 1), inside(q + dj, 15)))
    for d in range(4):
        greet(first, (s + 1, (x + d) % 4 * 8 + z))
        expect(second)
    greet(second, (s - 1, t))
    expect(first)
    for d in range(1, 4):
        greet(always, (s, (x + d) % 4 * 8 + z))
        expect(always)
    for mm in range(2):
        at = tm_of(mm, q)
        greet(jnp.logical_or(first, at != t), (2 * y + 1, at))
    for k in range(2):
        expect(second)
        expect(both(second, 2 * j + k != t))
    @pl.when(second)
    def _():
        for tap in range(27):
            pltpu.make_async_copy(k_hbm.at[tap], tap_block(WfB, tap), ownr).start()

    pl.semaphore_wait(entry, sum(expected))

    pl.when(base)(lambda: pltpu.make_async_copy(clips_hbm, clips, clr).wait())

    for dj in (2, 1, 0, -1):
        for mm in range(2):
            there = q + dj
            ok = both(both(second, y == CLIP_PLANE[dj]), inside(there, 15))
            to = tm_of(mm, there)
            slot = (2 - dj) * 2 + e
            if CLIP_PLANE[dj] == 0:
                send_or_copy(clips.at[mm], X0.at[slot], x0r.at[2 - dj], (1, to), ok, to == t)
            else:
                send(clips.at[mm], X0.at[slot], x0r.at[2 - dj], (1, to), ok)
    idx = len(drains)
    all_taps = lambda: remote(k_hbm, k_hbm, kr, (s + 1, t), idx)
    drains.append((first, all_taps))

    @pl.when(first)
    def _():
        for tap in range(27):
            remote(k_hbm.at[tap], tap_block(WfA, tap), kr, (s + 1, t), idx).start()

    for dj in (0, -1, -2):
        for mm in range(2):
            there = q + dj
            ok = both(both(first, y == PLANES - 1), both(there >= 0, there <= 15))
            send(cot.at[mm], G2.at[-2 * dj + e], g2r.at[-dj], (2 * PLANES - 1, tm_of(mm, there)), ok)

    def bwd_weight(dst, src):
        for tap in range(27):
            tap_block(dst, tap)[...] = tap_block(src, 26 - tap)[...].astype(F32).T.astype(BF16)

    def frame_silu(ref, k):
        return silu(ref[k].astype(F32)).astype(BF16)

    def build_patches(ref, TT):
        def one(k, carry):
            v = frame_silu(ref, k).astype(F32).reshape(16, 8, 128)
            for dw in range(3):
                vw = v if dw == 1 else shift_w(v, dw - 1)
                for dh in range(3):
                    vh = vw if dh == 1 else shift_h(vw, dh - 1)
                    TT[k, dh * 3 + dw] = vh.reshape(128, 128).T.astype(BF16)
            return carry

        lax.fori_loop(0, 4, one, 0)

    def take(k):
        for at in (k, k + 1):
            SX[at] = frame_silu(X0, at)

    def block_a(lo, hi):
        out = conv([SX[k] for k in range(lo, hi + 2)], WfA)
        for k in range(lo, hi):
            v = (X0[k + 2].astype(F32) + out[k - lo]).astype(BF16)
            X1[k] = v
            if k < 4:
                SB[k] = silu(v.astype(F32)).astype(BF16)

    def block_b():
        out = conv([SB[k] for k in range(4)], WfB)
        for k in range(2):
            X2[k] = (X1[k + 2].astype(F32) + out[k]).astype(BF16)

    def back_a(k):
        return conv([G2[at] for at in range(k, k + 4)], WbB)

    def grad_a(k, back):
        G1[k] = (G2[k].astype(F32) + back * S1[k]).astype(BF16)

    def out_home(src, dst, recv, core, cond):
        for k in range(2):
            dev = (2 * y + core, 2 * j + k)
            if core == 0:
                send(src.at[k], dst.at[m], recv.at[m], dev, cond)
            else:
                send_or_copy(src.at[k], dst.at[m], recv.at[m], dev, cond, 2 * j + k == t)

    @pl.when(second)
    def _():
        zero2 = jnp.zeros((2, 128, 128), BF16)

        @pl.when(j < 2)
        def _():
            X0[0:2] = zero2

        @pl.when(j < 1)
        def _():
            X0[2:4] = zero2

        @pl.when(j > 14)
        def _():
            X0[6:8] = zero2
            G2[2:4] = zero2

        @pl.when(j > 13)
        def _():
            G2[4:6] = zero2

        pltpu.make_async_copy(WfB, WfB, ownr).wait()
        arrive(WfA, kr)

        @pl.when(y > 2)
        def _():
            bwd_weight(WbB, WfB)
            bwd_weight(WbA, WfA)

        @pl.when(y == PLANES - 1)
        def _():
            arrive(G2.at[0:2], g2r.at[0])
            arrive_if(j <= 14, G2.at[2:4], g2r.at[1])
            arrive_if(j <= 13, G2.at[4:6], g2r.at[2])
            BK[0], BK[1] = back_a(0)
            BK[2], BK[3] = back_a(2)

        arrive_if(j >= 1, X0.at[2:4], x0r.at[1])
        take(2)

        @pl.when(y < PLANES - 1)
        def _():
            arrive_if(j >= 2, X0.at[0:2], x0r.at[0])
            take(0)
            block_a(0, 2)

        arrive(X0.at[4:6], x0r.at[2])
        take(4)
        block_a(2, 4)

        @pl.when(y < PLANES - 1)
        def _():
            block_b()

        @pl.when(y == PLANES - 1)
        def _():
            arrive_if(j <= 14, X0.at[6:8], x0r.at[3])
            take(6)
            block_a(4, 6)

    forward = both(second, y < PLANES - 1)
    fast = []

    def flush():
        while fast:
            cond, make = fast.pop()
            pl.when(cond)(lambda make=make: make().wait_send())

    def send_fast(src, dst, recv, dev, cond):
        send(src, dst, recv, dev, cond)
        fast.append(drains[-1])
        drains[-1] = None

    odd = j % 2 == 1
    even = j % 2 == 0
    for dj, when in ((1, odd), (2, None), (1, even), (0, None), (-1, y == PLANES - 2), (-1, y < PLANES - 2)):
        there = j + dj
        ok = both(forward, inside(there, 15))
        if when is not None:
            ok = both(ok, when)
        if len(fast) == 5:
            flush()
        send_fast(X2, X0.at[(2 - dj) * 2 : (2 - dj) * 2 + 2], x0r.at[2 - dj], (s + 2, tm_of(m, there)), ok)

    top = both(second, y == PLANES - 1)

    @pl.when(both(second, y <= 2))
    def _():
        bwd_weight(WbB, WfB)
        bwd_weight(WbA, WfA)

    @pl.when(both(second, y < PLANES - 1))
    def _():
        arrive_if(j <= 14, X0.at[6:8], x0r.at[3])
        take(6)
        block_a(4, 6)

    flush()
    behind = both(second, y > 0)
    lower = both(first, y > 0)
    ground = both(second, y == 0)
    send(X1.at[0:4], KX, kxr, (s + 2, t), forward)
    send(X0.at[2:6], KX, kxr, (s - 1, t), behind)

    def swap_patches(cond, TT, PX, pxr):
        for d in range(4):
            other = (x + d) % 4
            src = TT.at[:, :, pl.ds(pl.multiple_of(32 * other, 32), 32), :]
            if d == 0:
                pl.when(cond)(lambda: pltpu.make_async_copy(src, PX.at[x], pxr.at[0]).start())
            else:
                send(src, PX.at[x], pxr.at[d], (s, other * 8 + z), cond)

    @pl.when(ground)
    def _():
        build_patches(X0.at[2:6], TT)

    @pl.when(both(forward, y > 0))
    def _():
        arrive(KX, kxr)
        build_patches(KX, TT)

    swap_patches(forward, TT, PX, pxr)
    out_home(X1.at[2:4], act, acr, 0, forward)
    out_home(X2, act, acr, 1, forward)

    @pl.when(second)
    def _():
        for k in range(4):
            S1[k] = silu_slope(X1[k + 2].astype(F32))
        for k in range(2):
            S0[k] = silu_slope(X0[k + 4].astype(F32))

        @pl.when(y < PLANES - 1)
        def _():
            arrive_if(j <= 14, G2.at[2:4], g2r.at[1])
            arrive_if(j <= 13, G2.at[4:6], g2r.at[2])
            for k, back in zip((2, 3), back_a(2)):
                grad_a(k, back)
            arrive(G2.at[0:2], g2r.at[0])
            for k, back in zip((0, 1), back_a(0)):
                grad_a(k, back)

        @pl.when(y == PLANES - 1)
        def _():
            for k in range(4):
                grad_a(k, BK[k])

    def gather(src, GL, glr, cond):
        for d in (2, 1, 3):
            other = (x + d) % 4
            send(src, GL.at[x], glr.at[d], (s, other * 8 + z), cond)
        pl.when(cond)(lambda: pltpu.make_async_copy(src, GL.at[x], glr.at[0]).start())

    gather(G1.at[0:2], GL, glr, ground)

    @pl.when(second)
    def _():
        out = conv([G1[k] for k in range(4)], WbA)
        for k in range(2):
            G0[k] = (G1[k].astype(F32) + out[k] * S0[k]).astype(BF16)

    for dj, when in ((-1, even), (-2, None), (-1, odd), (0, None)):
        there = j + dj
        ok = both(both(second, y > 0), there >= 0)
        if when is not None:
            ok = both(ok, when)
        send_fast(G0, G2.at[-2 * dj : -2 * dj + 2], g2r.at[-dj], (s - 2, tm_of(m, there)), ok)
    flush()
    gather(G0, GL, glr, behind)
    for d in (2, 1, 3, 0):
        other = (x + d) % 4
        send(G1.at[0:2], GL.at[x], glr.at[d], (s - 1, other * 8 + z), behind)
    gather(G2.at[0:2], GL2, gl2r, top)
    out_home(G0, grad, grr, 0, behind)
    out_home(G1, grad, grr, 1, behind)

    @pl.when(top)
    def _():
        arrive_if(j >= 2, X0.at[0:2], x0r.at[0])
        take(0)
        block_a(0, 2)
        block_b()
        build_patches(X1, TT2)

    out_home(X1.at[2:4], act, acr, 0, top)
    out_home(X2, act, acr, 1, top)
    swap_patches(top, TT2, PX2, px2r)

    @pl.when(jnp.logical_or(lower, top))
    def _():
        arrive(KX, kxr)
        build_patches(KX, TT)

    swap_patches(jnp.logical_or(lower, top), TT, PX, pxr)

    def taps_of(k):
        return pl.ds(7 * (k % 4), 7)

    def reduce_terms(cond, PX, GL, RS, RL, pxr, glr, rsr, out, between=lambda: None):
        @pl.when(cond)
        def _():
            for d in range(4):
                source = (x + 4 - d) % 4
                arrive(PX.at[source], pxr.at[d])
                arrive(GL.at[source], glr.at[d])
            for dt in range(3):
                total = None
                for p in range(4):
                    left = jnp.concatenate(
                        [PX[p, dt].reshape(288, 128), PX[p, dt + 1].reshape(288, 128)], axis=1
                    )
                    term = jnp.dot(left, GL[p].reshape(256, 128), preferred_element_type=F32)
                    total = term if total is None else total + term
                RS[dt * 9 : (dt + 1) * 9] = total.astype(BF16).reshape(9, 2, 16, 128)
            RS[27] = jnp.zeros((2, 16, 128), BF16)

        for d in (4, 3, 5, 2, 6, 1, 7):
            other = (z + d) % 8
            send(RS.at[taps_of(other), other // 4], RL.at[z], rsr.at[d], (s, x * 8 + other), cond)
        between()

        @pl.when(cond)
        def _():
            total = RS[taps_of(z), z // 4].astype(F32)
            for d in range(1, 8):
                source = (z + 8 - d) % 8
                arrive(RL.at[source], rsr.at[d])
                total = total + RL[source].astype(F32)
            out[...] = total.astype(BF16)

    right, left, far = (x + 1) % 4, (x + 3) % 4, (x + 2) % 4
    order = (0, 1, 7, 2, 6, 3, 5, 4)

    def piece(ref, row, d):
        k = (z + 8 - d) % 8
        return ref.at[taps_of(k), 2 * row + k // 4]

    def pass_on(buf, row, d, recv, dev):
        send(piece(buf, row, d), piece(buf, row, d), recv, dev, second)

    def hand_over(row, d):
        send(piece(AG, row, d), piece(kg, row, d), kgr, (s - 1, t), second)

    def along_z(buf, azr):
        for d in (4, 3, 5, 2, 6, 1, 7):
            pass_on(buf, x, 0, azr.at[d], (s, x * 8 + (z + d) % 8))

    def along_x(buf, azr, axr):
        for d in order:
            if d:
                arrive_if(second, piece(buf, x, d), azr.at[d])
            pass_on(buf, x, d, axr.at[0, d], (s, right * 8 + z))
            pass_on(buf, x, d, axr.at[1, d], (s, left * 8 + z))

    def further_x(buf, axr):
        for at, d in enumerate(order):
            arrive_if(second, piece(buf, left, d), axr.at[0, d])
            arrive_if(second, piece(buf, right, d), axr.at[1, d])
            if at % 2:
                pass_on(buf, left, d, axr.at[2, d], (s, right * 8 + z))
            else:
                pass_on(buf, right, d, axr.at[2, d], (s, left * 8 + z))

    mine = piece(kg, x, 0)
    even_sum = piece(AG, x, 0)
    def last_home():
        out_home(G0, grad, grr, 0, ground)
        out_home(G1, grad, grr, 1, ground)

    reduce_terms(s > 0, PX, GL, RS, RL, pxr, glr, rsr, CH, last_home)
    send(CH, mine, chr, (s - 2, t), behind)
    send(CH, even_sum, evr, (s + 1, t), lower)

    @pl.when(ground)
    def _():
        even_sum[...] = CH[...]

    arrive_if(behind, even_sum, evr)
    along_z(AG, azr)
    reduce_terms(top, PX2, GL2, RS2, RL2, px2r, gl2r, rs2r, mine)
    arrive_if(forward, mine, chr)
    along_z(kg, az2r)
    along_x(AG, azr, axr)
    along_x(kg, az2r, ax2r)
    further_x(AG, axr)
    further_x(kg, ax2r)
    for row in (x, left, right):
        for d in order:
            hand_over(row, d)
    for d in order:
        arrive_if(second, piece(AG, far, d), axr.at[2, d])
        hand_over(far, d)
    for d in order:
        arrive_if(second, piece(kg, far, d), ax2r.at[2, d])
    arrive_if(first, kg, kgr)
    for mm in range(2):
        arrive(act.at[mm], acr.at[mm])
        arrive(grad.at[mm], grr.at[mm])
    for cond, make in filter(None, drains):
        if cond is None:
            make().wait_send()
        else:
            pl.when(cond)(lambda make=make: make().wait_send())


def body(clips, kernels, cotangent):
    micro, frames, height, width, chan = clips.shape
    vmem = pl.BlockSpec(memory_space=pltpu.VMEM)
    frame = lambda n: pltpu.VMEM((n, 128, 128), BF16)
    weight = pltpu.VMEM((384, 1152), BF16)
    dma = pltpu.SemaphoreType.DMA
    terms = (
        pltpu.VMEM((4, 9, 128, 128), BF16),
        pltpu.VMEM((4, 4, 9, 32, 128), BF16),
        pltpu.VMEM((4, 2, 128, 128), BF16),
        pltpu.VMEM((28, 2, 16, 128), BF16),
        pltpu.VMEM((8, 7, 16, 128), BF16),
    )
    act, grad, kg = pl.pallas_call(
        kernel,
        out_shape=(
            jax.ShapeDtypeStruct((2, 128, 128), BF16),
            jax.ShapeDtypeStruct((2, 128, 128), BF16),
            jax.ShapeDtypeStruct((28, 8, 16, 128), BF16),
        ),
        in_specs=[pl.BlockSpec(memory_space=pltpu.HBM)] * 3,
        out_specs=(vmem,) * 3,
        scratch_shapes=[
            frame(8), frame(6), frame(2), frame(6), frame(4), frame(2),
            pltpu.VMEM((4, 128, 128), F32),
            pltpu.VMEM((4, 128, 128), F32),
            pltpu.VMEM((2, 128, 128), F32),
            frame(8), frame(4), frame(2), weight, weight, weight, weight, frame(4), pltpu.VMEM((28, 8, 16, 128), BF16), pltpu.VMEM((7, 16, 128), BF16),
            *terms, *terms,
            dma((220,)), dma, dma, dma((4,)), dma((3,)), dma, dma, dma((2,)), dma((2,)),
            dma((4,)), dma((4,)), dma((8,)), dma((4,)), dma((4,)), dma((8,)),
            dma, dma, dma, dma((8,)), dma((3, 8)), dma((8,)), dma((3, 8)),
        ],
        compiler_params=pltpu.CompilerParams(
            collective_id=0, has_side_effects=True, vmem_limit_bytes=60 << 20,
        ),
        name="blocks",
    )(
        clips.reshape(2, 128, 128),
        kernels.reshape(27, 128, 128),
        cotangent.reshape(2, 128, 128),
    )
    total = micro * frames * lax.axis_size("tm") * height * width
    norm = 1.0 / jnp.sqrt(jnp.float32(total))
    parts = kg[:27].reshape(27, chan, chan).astype(F32) * norm
    return (
        act.reshape(1, micro, 1, height, width, chan),
        grad.reshape(1, micro, 1, height, width, chan),
        parts.reshape(1, 3, 3, 3, chan, chan),
    )


def solution(mesh):
    placed = (
        P(None, "tm", None, None, None),
        P("section", None, None, None, None, None),
        P(None, "tm", None, None, None),
    )
    return jax.shard_map(
        body,
        mesh=mesh,
        in_specs=placed,
        out_specs=(
            P("section", None, "tm", None, None, None),
            P("section", None, "tm", None, None, None),
            P("section", None, None, None, None, None),
        ),
        check_vma=False,
    )
```
